32 devices in a mesh: dom: 32 (over z, y, x, core).
Axes of the slice: x: 2, y: 2, z: 4, core: 2. Of those that a mesh axis runs over, the one named last changes fastest.
Arguments:
- dofs: float32 [56, 9, 4096], P(None, None, 'dom'), may hold values from -6 to 6
- star: float32 [3, 9, 9, 4096], P(None, None, None, 'dom'), may hold values from -8 to 8
- flux_minus: float32 [4, 9, 9, 4096], P(None, None, None, 'dom'), may hold values from -0.4 to 0.4
- flux_plus: float32 [4, 9, 9, 4096], P(None, None, None, 'dom'), may hold values from -0.4 to 0.4
- cohesion: float32 [4096], P('dom'), may hold values from 0.5 to 4
- stiff: float32 [3, 56, 56], replicated, may hold values from -1 to 1
- face_proj: float32 [4, 21, 56], replicated, may hold values from -0.75 to 0.75
- lift: float32 [4, 56, 21], replicated, may hold values from -1.25 to 1.25
- rotate: float32 [3, 21, 21], replicated, may hold values from -1.25 to 1.25
- cluster: int32 [4096], P('dom'), may hold values from 0 to 1, as said below
- neighbor: int32 [4, 4096], P(None, 'dom'), may hold values from 0 to 256, as said below
- neigh_face: int32 [4, 4096], P(None, 'dom'), may hold values from 0 to 3, as said below
- orient: int32 [4, 4096], P(None, 'dom'), may hold values from 0 to 2, as said below
- send_elem: int32 [4, 1024], P(None, 'dom'), may hold values from 0 to 127, as said below
- send_face: int32 [4, 1024], P(None, 'dom'), may hold values from 0 to 3, as said below
Outputs:
- new_dofs: float32 [56, 9, 4096], P(None, None, 'dom')
The draws below stay inside these ranges and needn't reach their ends.
Inputs may be any that keep to these rules, and one draw needn't show every extreme that they name: `cluster`: each partition has at most 64 fine elements, and it has at most 96 together with the partition half the axis away; both bounds are reached in every draw. `neighbor`: values below 128 name an element of the same partition; 128 + b * 32 + s names slot s of the faces shared with the partition at offset -2, -1, 1, 2 for b = 0, 1, 2, 3, that is slot s of block 3 - b in that partition's send_elem and send_face; 256 marks the mesh's boundary. Every slot of an existing partition is named by exactly one face, and faces pair symmetrically. `neigh_face`: the neighbour's face across each face; for a shared slot it equals the slot's send_face; 0 on the boundary. `orient`: 0 on the boundary; a face pair's codes h and (3 - h) % 3. `send_elem`: block b holds, for slot s, the local element whose face the partition shares with the partition at offset -2, -1, 1, 2 for b = 0, 1, 2, 3. `send_face`: the face of that element in slot s of block b.
All inputs are finite; a program needn't handle non-finite values.
Results may differ from the reference program's by a relative error of at most 0.00024.
Values sent between devices are 32-bit elements; how exact they have to be, the bound alone decides.
A program may use at most 128 MiB of HBM per device.

```python
import math
import jax
import jax.numpy as jnp
from jax import lax

BASIS = 56
FACE_BASIS = 21
QUANT = 9
ORDER = 6
RATE = 4
ELEM_DEV = 128
SLOTS = 32
FINE_CAP = 64
PAIR_CAP = 96
ELEMENTS = 4096
N_DOM = 32


def mesh_tables(key):
    devices = ELEMENTS // ELEM_DEV
    local_faces = 4 * ELEM_DEV
    crossing = 4 * SLOTS
    boundary = ELEM_DEV + 4 * SLOTS
    base = jax.random.fold_in(key, 4411)
    perm_key, cross_key, inner_key = jax.random.split(base, 3)
    orders = jax.vmap(lambda single: jax.random.permutation(single, local_faces))(jax.random.split(perm_key, devices)).astype(jnp.int32)
    cross_turn = jax.random.randint(cross_key, (devices, 2, SLOTS), 0, 3, dtype=jnp.int32)
    inner_pairs = (local_faces - crossing) // 2
    inner_turn = jax.random.randint(inner_key, (devices, inner_pairs), 0, 3, dtype=jnp.int32)
    partner = jnp.full((devices, local_faces), boundary, jnp.int32)
    across = jnp.zeros((devices, local_faces), jnp.int32)
    turning = jnp.zeros((devices, local_faces), jnp.int32)
    device_rows = jnp.arange(devices, dtype=jnp.int32)[:, None]
    first_half = orders[:, crossing::2]
    second_half = orders[:, crossing + 1::2]
    partner = partner.at[device_rows, first_half].set(second_half // 4)
    partner = partner.at[device_rows, second_half].set(first_half // 4)
    across = across.at[device_rows, first_half].set(second_half % 4)
    across = across.at[device_rows, second_half].set(first_half % 4)
    turning = turning.at[device_rows, first_half].set(inner_turn)
    turning = turning.at[device_rows, second_half].set((3 - inner_turn) % 3)
    slot_ids = jnp.arange(SLOTS, dtype=jnp.int32)[None, :]
    for step_size in (1, 2):
        upper = 1 + step_size
        lower = 2 - step_size
        upward = orders[:, upper * SLOTS:(upper + 1) * SLOTS]
        downward = orders[:, lower * SLOTS:(lower + 1) * SLOTS]
        turn_up = cross_turn[:, step_size - 1, :]
        has_up = device_rows + step_size < devices
        has_down = device_rows - step_size >= 0
        from_up = jnp.roll(downward, -step_size, axis=0)
        from_down = jnp.roll(upward, step_size, axis=0)
        turn_down = jnp.roll(turn_up, step_size, axis=0)
        partner = partner.at[device_rows, upward].set(jnp.where(has_up, ELEM_DEV + upper * SLOTS + slot_ids, boundary))
        across = across.at[device_rows, upward].set(jnp.where(has_up, from_up % 4, 0))
        turning = turning.at[device_rows, upward].set(jnp.where(has_up, turn_up, 0))
        partner = partner.at[device_rows, downward].set(jnp.where(has_down, ELEM_DEV + lower * SLOTS + slot_ids, boundary))
        across = across.at[device_rows, downward].set(jnp.where(has_down, from_down % 4, 0))
        turning = turning.at[device_rows, downward].set(jnp.where(has_down, (3 - turn_down) % 3, 0))
    sending = orders[:, :crossing].reshape(devices, 4, SLOTS)
    return (partner, across, turning, sending // 4, sending % 4)


def to_faces(table):
    return jnp.transpose(table.reshape(-1, ELEM_DEV, 4), (2, 0, 1)).reshape(4, -1).astype(jnp.int32)


def to_slots(table):
    return jnp.transpose(table, (1, 0, 2)).reshape(4, -1).astype(jnp.int32)


def draw_neighbor(key, part):
    return to_faces(mesh_tables(key)[0])


def draw_neigh_face(key, part):
    return to_faces(mesh_tables(key)[1])


def draw_orient(key, part):
    return to_faces(mesh_tables(key)[2])


def draw_send_elem(key, part):
    return to_slots(mesh_tables(key)[3])


def draw_send_face(key, part):
    return to_slots(mesh_tables(key)[4])


def draw_cluster(key, part):
    devices = ELEMENTS // ELEM_DEV
    pair_count = devices // 2
    base = jax.random.fold_in(key, 9127)
    total_key, spare_key, flip_key, rank_key = jax.random.split(base, 4)
    totals = jax.random.randint(total_key, (pair_count,), ELEM_DEV // 8, PAIR_CAP + 1, dtype=jnp.int32)
    totals = totals.at[0].set(PAIR_CAP)
    spare = jax.random.randint(spare_key, (pair_count,), 0, ELEM_DEV, dtype=jnp.int32) % (totals // 4 + 1)
    busy = jnp.minimum(FINE_CAP, totals - spare)
    quiet = totals - busy
    flipped = jax.random.randint(flip_key, (pair_count,), 0, 2, dtype=jnp.int32)
    lower_count = jnp.where(flipped == 1, busy, quiet)
    upper_count = jnp.where(flipped == 1, quiet, busy)
    counts = jnp.concatenate([lower_count, upper_count])
    ranks = jax.vmap(lambda single: jax.random.permutation(single, ELEM_DEV))(jax.random.split(rank_key, devices))
    return (ranks < counts[:, None]).astype(jnp.int32).reshape(-1)


def draw_star(key, part):
    labels = draw_cluster(key, part)
    star_key = jax.random.fold_in(key, 5233)
    raw = jax.random.normal(star_key, (3, QUANT, QUANT, ELEMENTS), jnp.float32)
    values = jnp.clip(0.35 * raw, -2.0, 2.0)
    factor = jnp.where(labels == 1, 4.0, 1.0).astype(jnp.float32)
    return (values * factor[None, None, None, :]).astype(jnp.float32)


def levels(stream_key, shape, cuts, low, high):
    loudness = 1.0
    for position, shards_of in cuts:
        draws = jax.random.uniform(jax.random.fold_in(jax.random.fold_in(stream_key, 6), position), (shards_of,), jnp.float32, low / len(cuts), high / len(cuts))
        loudness = loudness * jnp.repeat(jnp.exp(draws), shape[position] // shards_of).reshape((-1,) + (1,) * (len(shape) - 1 - position))
    return loudness


def gaussian(own_key, shape, spread, most, shards=(), kind=jnp.bfloat16):
    values = spread * jax.random.normal(own_key, shape, jnp.float32)
    if shards:
        values = values * levels(own_key, shape, shards, -0.22, 0.18)
    return jnp.clip(values, -most, most).astype(kind)


def setup_inputs(seed: int = 0) -> dict:
    keys = jax.random.split(jax.random.key(seed), 16)
    return {
        "dofs": gaussian(keys[0], (BASIS, QUANT, ELEMENTS), 1.0, 6.0, ((2, 32),), jnp.float32),
        "star": draw_star(jax.random.fold_in(keys[15], 71), 0),
        "flux_minus": gaussian(keys[2], (4, QUANT, QUANT, ELEMENTS), 0.05, 0.4, ((3, 32),), jnp.float32),
        "flux_plus": gaussian(keys[3], (4, QUANT, QUANT, ELEMENTS), 0.05, 0.4, ((3, 32),), jnp.float32),
        "cohesion": jnp.clip(jnp.exp(math.log(4.0) - 2.0794415 * jax.random.uniform(keys[4], (ELEMENTS,), jnp.float32) ** levels(keys[4], (ELEMENTS,), ((0, 32),), -0.2, 0.2)), 0.5, 4.0),
        "stiff": gaussian(keys[5], (3, BASIS, BASIS), (BASIS // 2) ** -0.5, 1.0, (), jnp.float32),
        "face_proj": gaussian(keys[6], (4, FACE_BASIS, BASIS), BASIS ** -0.5, 0.75, (), jnp.float32),
        "lift": gaussian(keys[7], (4, BASIS, FACE_BASIS), FACE_BASIS ** -0.5, 1.25, (), jnp.float32),
        "rotate": gaussian(keys[8], (3, FACE_BASIS, FACE_BASIS), FACE_BASIS ** -0.5, 1.25, (), jnp.float32),
        "cluster": draw_cluster(jax.random.fold_in(keys[15], 71), 0),
        "neighbor": draw_neighbor(jax.random.fold_in(keys[15], 71), 0),
        "neigh_face": draw_neigh_face(jax.random.fold_in(keys[15], 71), 0),
        "orient": draw_orient(jax.random.fold_in(keys[15], 71), 0),
        "send_elem": draw_send_elem(jax.random.fold_in(keys[15], 71), 0),
        "send_face": draw_send_face(jax.random.fold_in(keys[15], 71), 0),
    }


PRECISE = lax.Precision.HIGHEST

def prepare(stiff, star):
    skew = 0.5 * (stiff - jnp.transpose(stiff, (0, 2, 1)))
    sym = 0.5 * (star + jnp.transpose(star, (0, 2, 1, 3)))
    return (skew, sym)

def operator_left(skew, transposed):
    basis_size = skew.shape[1]
    order_axes = (2, 0, 1) if transposed else (1, 0, 2)
    return jnp.transpose(skew, order_axes).reshape(basis_size, 3 * basis_size)

def star_apply(matrices, values):
    running = jnp.expand_dims(matrices[..., 0, :], -3) * values[..., 0:1, :]
    for column in range(1, values.shape[-2]):
        running = running + jnp.expand_dims(matrices[..., column, :], -3) * values[..., column:column + 1, :]
    return running

def apply_operator(values, left_matrix, sym):
    stacked = jnp.stack([star_apply(sym[direction], values) for direction in range(3)])
    product = jnp.dot(left_matrix, stacked.reshape(left_matrix.shape[1], -1), precision=PRECISE)
    return product.reshape(values.shape)

def derivatives(values, left_matrix, sym):
    series = [values]
    for term in range(ORDER - 1):
        series.append(-apply_operator(series[-1], left_matrix, sym))
    return series

def interval_weights(begin_time, end_time):
    return [(end_time ** (term + 1) - begin_time ** (term + 1)) / math.factorial(term + 1) for term in range(ORDER)]

def integrate(series, weights):
    running = weights[0] * series[0]
    for term in range(1, ORDER):
        running = running + weights[term] * series[term]
    return running

def traces(values, face_proj):
    face_count, fbasis, basis_size = face_proj.shape
    product = jnp.dot(face_proj.reshape(face_count * fbasis, basis_size), values.reshape(basis_size, -1), precision=PRECISE)
    return product.reshape(face_count, fbasis, values.shape[1], values.shape[2])

def lift_apply(face_values, lift):
    face_count, basis_size, fbasis = lift.shape
    left_matrix = jnp.transpose(lift, (1, 0, 2)).reshape(basis_size, face_count * fbasis)
    product = jnp.dot(left_matrix, face_values.reshape(face_count * fbasis, -1), precision=PRECISE)
    return product.reshape(basis_size, face_values.shape[2], face_values.shape[3])

def rotate_apply(face_values, orient, rotate):
    turned = jnp.einsum('kij,fjqm->kfiqm', rotate, face_values, precision=PRECISE)
    rotation = orient[:, None, None, :]
    return jnp.where(rotation == 0, turned[0], jnp.where(rotation == 1, turned[1], turned[2]))

def plastic(values, cohesion):
    average = values[0]
    mean_stress = (average[0] + average[1] + average[2]) / 3.0
    dev_xx = average[0] - mean_stress
    dev_yy = average[1] - mean_stress
    dev_zz = average[2] - mean_stress
    second = 0.5 * (dev_xx * dev_xx + dev_yy * dev_yy + dev_zz * dev_zz) + average[3] * average[3] + average[4] * average[4] + average[5] * average[5]
    factor = cohesion / jnp.maximum(jnp.sqrt(second), cohesion)
    pressure = (values[:, 0] + values[:, 1] + values[:, 2]) / 3.0
    normal = pressure[:, None, :] + factor * (values[:, 0:3, :] - pressure[:, None, :])
    shear_part = factor * values[:, 3:6, :]
    return jnp.concatenate([normal, shear_part, values[:, 6:, :]], axis=1)

def update(values, predictor, own_faces, remote_faces, orient, back_left, sym, flux_minus, flux_plus, cohesion, lift, rotate):
    volume_term = apply_operator(predictor, back_left, sym)
    local_term = lift_apply(star_apply(flux_minus, own_faces), lift)
    remote_term = lift_apply(star_apply(flux_plus, rotate_apply(remote_faces, orient, rotate)), lift)
    return plastic(values + volume_term - local_term - remote_term, cohesion)

def flatten_faces(face_values):
    face_count, fbasis, quantities, columns = face_values.shape
    return jnp.transpose(face_values, (0, 3, 1, 2)).reshape(face_count * columns, fbasis * quantities)

def lookup(face_values, face_ids, targets, usable):
    face_count, fbasis, quantities, columns = face_values.shape
    flattened = flatten_faces(face_values)
    picked = jnp.take(flattened, (face_ids * columns + targets).reshape(-1), axis=0)
    picked = jnp.where(usable.reshape(-1)[:, None], picked, 0.0)
    return jnp.transpose(picked.reshape(face_count, -1, fbasis, quantities), (0, 2, 3, 1))

def reference(dofs, star, flux_minus, flux_plus, cohesion, stiff, face_proj, lift, rotate, cluster, neighbor, neigh_face, orient, send_elem, send_face):
    skew, sym = prepare(stiff, star)
    forward_left = operator_left(skew, False)
    back_left = operator_left(skew, True)
    elements = dofs.shape[2]
    device_of = jnp.arange(elements, dtype=jnp.int32) // ELEM_DEV
    ghost_offset = neighbor - ELEM_DEV
    is_local = neighbor < ELEM_DEV
    is_ghost = (ghost_offset >= 0) & (ghost_offset < 4 * SLOTS)
    usable = is_local | is_ghost
    block = jnp.clip(ghost_offset // SLOTS, 0, 3).astype(jnp.int32)
    slot_id = jnp.clip(ghost_offset % SLOTS, 0, SLOTS - 1).astype(jnp.int32)
    offset_table = jnp.array([-2, -1, 1, 2], dtype=jnp.int32)
    source = jnp.clip(device_of[None, :] + offset_table[block], 0, N_DOM - 1).astype(jnp.int32)
    sender_elem = send_elem[3 - block, source * SLOTS + slot_id]
    sender_face = send_face[3 - block, source * SLOTS + slot_id]
    local_target = device_of[None, :] * ELEM_DEV + jnp.clip(neighbor, 0, ELEM_DEV - 1)
    targets = jnp.where(is_local, local_target, source * ELEM_DEV + sender_elem)
    targets = jnp.where(usable, targets, 0).astype(jnp.int32)
    face_ids = jnp.where(is_local, neigh_face, sender_face).astype(jnp.int32)
    fine = (cluster == 1)[None, None, :]
    series = derivatives(dofs, forward_left, sym)
    full = integrate(series, interval_weights(0.0, 1.0))
    pieces = [integrate(series, interval_weights(substep / RATE, (substep + 1) / RATE)) for substep in range(RATE)]
    fine_weights = interval_weights(0.0, 1.0 / RATE)
    state_fine = dofs
    accumulated = pieces[0]
    for substep in range(RATE):
        if substep == 0:
            predictor = pieces[0]
        else:
            own_pred = integrate(derivatives(state_fine, forward_left, sym), fine_weights)
            predictor = jnp.where(fine, own_pred, pieces[substep])
            accumulated = accumulated + predictor
        face_values = traces(predictor, face_proj)
        remote = lookup(face_values, face_ids, targets, usable)
        stepped = update(state_fine, predictor, face_values, remote, orient, back_left, sym, flux_minus, flux_plus, cohesion, lift, rotate)
        state_fine = jnp.where(fine, stepped, state_fine)
    remote_all = lookup(traces(accumulated, face_proj), face_ids, targets, usable)
    coarse = update(dofs, full, traces(full, face_proj), remote_all, orient, back_left, sym, flux_minus, flux_plus, cohesion, lift, rotate)
    return jnp.where(fine, state_fine, coarse)
```

```python
import functools
import math

import jax
import jax.numpy as jnp
import numpy as np
from jax import lax
from jax.experimental import pallas as pl
from jax.experimental.pallas import tpu as pltpu
from jax.sharding import PartitionSpec as P

ORDER = 6
RATE = 4
OFFSETS = (-2, -1, 1, 2)
F32 = jnp.float32
BF16 = jnp.bfloat16


def round_up(value, multiple):
    return -(-value // multiple) * multiple


def interval_weights(begin_time, end_time):
    return [
        (end_time ** (term + 1) - begin_time ** (term + 1)) / math.factorial(term + 1)
        for term in range(ORDER)
    ]


def high(values):
    return values.astype(BF16).astype(F32)


def mm(left, right):
    return jnp.dot(left, right, preferred_element_type=F32)


def kernel(
    devices,
    dims,
    weight_ref,
    dofs_ref,
    star_ref,
    minus_ref,
    plus_ref,
    cohesion_ref,
    fine_ref,
    neighbor_ref,
    face_ref,
    orient_ref,
    slot_ref,
    main_in,
    turned_in,
    lift_in,
    out_ref,
    sym_ref,
    main_ref,
    turned_ref,
    lift_high,
    lift_low,
    onehot_local,
    onehot_ghost,
    onehot_send,
    state,
    pieces,
    pred,
    rhs,
    ya,
    yb,
    own_trace,
    turned,
    remote,
    flux,
    base,
    send,
    recv,
    send_sem,
    recv_sem,
):
    basis, quant, elems, fpad, faces, slots = dims
    bpad = round_up(basis, 16)
    rows = 3 * basis
    group = 3
    groups = quant // group
    width = group * elems
    frows = faces * fpad
    trows = quant * fpad
    seg = basis
    me = lax.axis_index("dom")

    def exists(position):
        other = me + OFFSETS[position]
        return (other >= 0) & (other < devices)

    barrier = pltpu.get_barrier_semaphore()
    for position in range(4):

        @pl.when(exists(position))
        def _():
            pl.semaphore_signal(
                barrier,
                inc=1,
                device_id=(me + OFFSETS[position],),
                device_id_type=pl.DeviceIdType.MESH,
            )

    def col(q):
        return slice(q * elems, (q + 1) * elems)

    def gcol(g):
        return slice(g * width, (g + 1) * width)

    for c in range(3):
        for q in range(quant):
            for p in range(q, quant):
                both = 0.5 * (star_ref[c, q, p : p + 1, :] + star_ref[c, p, q : q + 1, :])
                sym_ref[c, q, p : p + 1, :] = both
                if p != q:
                    sym_ref[c, p, q : q + 1, :] = both

    def split_left(ref):
        whole = ref[...]
        top = high(whole)
        lane = lax.broadcasted_iota(jnp.int32, whole.shape, 1)
        return jnp.where(lane < 2 * bpad, top, whole - top).astype(BF16)

    main_ref[...] = split_left(main_in)
    turned_ref[...] = split_left(turned_in)
    lift_whole = lift_in[...]
    lift_top = high(lift_whole)
    lift_high[...] = lift_top.astype(BF16)
    lift_low[...] = (lift_whole - lift_top)[:, 0:frows].astype(BF16)

    def onehot(row_count, index):
        ids = lax.broadcasted_iota(jnp.int32, (row_count, index.shape[1]), 0)
        return jnp.where(ids == index, 1.0, 0.0).astype(BF16)

    for f in range(faces):
        target = neighbor_ref[f : f + 1, :]
        across = face_ref[f : f + 1, :]
        local = jnp.where(target < elems, across * elems + target, -1)
        onehot_local[:, f * elems : (f + 1) * elems] = onehot(faces * elems, local)
        onehot_ghost[:, f * elems : (f + 1) * elems] = onehot(4 * slots, target - elems)
    onehot_send[...] = onehot(faces * elems, slot_ref[...])

    fine = fine_ref[...] == 1

    def put(q, values):
        top = high(values)
        pad = jnp.zeros((bpad - basis, elems), F32)
        upper = jnp.concatenate([values, pad], axis=0).astype(BF16)
        lower = jnp.concatenate([values - top, pad], axis=0).astype(BF16)
        rhs[0:bpad, col(q)] = upper
        rhs[bpad : 2 * bpad, col(q)] = lower
        rhs[2 * bpad : 3 * bpad, col(q)] = upper

    skew_rows = round_up(rows, 16)

    def product(g, target):
        result = mm(main_ref[0:skew_rows, :], rhs[:, gcol(g)])
        target[:, gcol(g)] = result[0:rows]

    def stage(source, target, emit):
        for g in range(groups):
            sums = [None] * group
            for c in range(3):
                for p in range(quant):
                    values = source[c * basis : (c + 1) * basis, col(p)]
                    for i in range(group):
                        term = sym_ref[c, g * group + i, p : p + 1, :] * values
                        sums[i] = term if sums[i] is None else sums[i] + term
            for i in range(group):
                emit(g * group + i, sums[i])
                if target is not None:
                    put(g * group + i, sums[i])
            if target is not None:
                product(g, target)

    def series(emit):
        for g in range(groups):
            for i in range(group):
                q = g * group + i
                emit(0, q, state[:, col(q)])
                put(q, state[:, col(q)])
            product(g, ya)

        def pair(j, carry):
            stage(ya, yb, functools.partial(emit, 2 * j + 1))
            stage(yb, ya, functools.partial(emit, 2 * j + 2))
            return carry

        lax.fori_loop(0, 2, pair, 0)
        stage(ya, None, functools.partial(emit, 5))

    def copy_of(step, position):
        return pltpu.make_async_remote_copy(
            src_ref=send.at[step, position],
            dst_ref=recv.at[step, 3 - position],
            send_sem=send_sem.at[step, position],
            recv_sem=recv_sem.at[step, 3 - position],
            device_id=(me + OFFSETS[position],),
            device_id_type=pl.DeviceIdType.MESH,
        )

    lane_seg = lax.broadcasted_iota(jnp.int32, (seg, 4 * slots), 1) // slots

    def repack(parts):
        made = []
        for b in range(4):
            value = parts[0] if b == 0 else pltpu.roll(parts[0], (4 - b) * slots, 1)
            for j in range(1, 4):
                shift = ((j - b) % 4) * slots
                moved = parts[j] if shift == 0 else pltpu.roll(parts[j], shift, 1)
                value = jnp.where(lane_seg == j, moved, value)
            made.append(value)
        return made

    def two_halves(values):
        top = high(values)
        return top.astype(BF16), (values - top).astype(BF16)

    def exchange(step, first, last):
        for g in range(groups):
            for i in range(group):
                q = g * group + i
                put(q, pieces[0, :, col(q)] if first else pred[:, col(q)])
            result = mm(turned_ref[...], rhs[:, gcol(g)])
            for i in range(group):
                q = g * group + i
                for f in range(faces):
                    code = orient_ref[f : f + 1, :]
                    options = [
                        result[
                            k * frows + f * fpad : k * frows + (f + 1) * fpad,
                            i * elems : (i + 1) * elems,
                        ]
                        for k in range(3)
                    ]
                    turned[q * fpad : (q + 1) * fpad, f * elems : (f + 1) * elems] = jnp.where(
                        code == 0, options[0], jnp.where(code == 1, options[2], options[1])
                    )
        top, low = two_halves(turned[...])
        sending = mm(top, onehot_send[...]) + mm(low, onehot_send[...])
        parts = [sending[j * seg : (j + 1) * seg] for j in range(4)]
        for b, value in enumerate(repack(parts)):
            send[step, b] = value
        if first:
            peers = sum(exists(position).astype(jnp.int32) for position in range(4))
            pl.semaphore_wait(barrier, peers)
        for position in range(4):

            @pl.when(exists(position))
            def _():
                copy_of(step, position).start()

        remote[...] = mm(top, onehot_local[...]) + mm(low, onehot_local[...])
        if first:
            for q in range(quant):
                whole = pieces[0, :, col(q)]
                for other in range(1, RATE):
                    whole = whole + pieces[other, :, col(q)]
                put(q, jnp.where(fine, pieces[0, :, col(q)], whole))
        for g in range(groups):
            result = mm(main_ref[...], rhs[:, gcol(g)])
            ya[:, gcol(g)] = result[0:rows]
            own_trace[:, gcol(g)] = result[rows : rows + frows]

        def volume(q, value):
            if not first:
                value = jnp.where(fine, value, 0.0)
            base[:, col(q)] = state[:, col(q)] + value

        stage(ya, None, volume)

        def solver(matrix_ref, f, g, load):
            sums = [None] * group
            for p in range(quant):
                values = load(p)
                for i in range(group):
                    term = matrix_ref[f, g * group + i, p : p + 1, :] * values
                    sums[i] = term if sums[i] is None else sums[i] + term
            return sums

        for f in range(faces):
            frange = slice(f * fpad, (f + 1) * fpad)
            for g in range(groups):
                sums = solver(minus_ref, f, g, lambda p: own_trace[frange, col(p)])
                for i in range(group):
                    value = sums[i] if first else jnp.where(fine, sums[i], 0.0)
                    flux[frange, col(g * group + i)] = value
        for position in range(4):

            @pl.when(exists(position))
            def _():
                copy_of(step, 3 - position).wait_recv()

        ghosts = repack([recv[step, b] for b in range(4)])
        ghost = jnp.concatenate(ghosts, axis=0)
        top, low = two_halves(ghost)
        remote[...] += mm(top, onehot_ghost[...]) + mm(low, onehot_ghost[...])
        for f in range(faces):
            frange = slice(f * fpad, (f + 1) * fpad)
            for g in range(groups):
                sums = solver(
                    plus_ref,
                    f,
                    g,
                    lambda p: remote[p * fpad : (p + 1) * fpad, f * elems : (f + 1) * elems],
                )
                for i in range(group):
                    flux[frange, col(g * group + i)] += sums[i]
        for g in range(groups):
            top, low = two_halves(flux[:, gcol(g)])
            lifted = mm(lift_high[...], jnp.concatenate([top, low], axis=0)) + mm(
                lift_low[...], top
            )
            base[:, gcol(g)] = base[:, gcol(g)] - lifted[0:basis]
        s = [base[0:1, col(q)] for q in range(6)]
        mean = (s[0] + s[1] + s[2]) / 3.0
        d = [s[i] - mean for i in range(3)]
        second = (
            0.5 * (d[0] * d[0] + d[1] * d[1] + d[2] * d[2])
            + s[3] * s[3]
            + s[4] * s[4]
            + s[5] * s[5]
        )
        cohesion = cohesion_ref[...]
        factor = cohesion / jnp.maximum(jnp.sqrt(second), cohesion)
        if last is not True:
            factor = jnp.where(fine | last, factor, 1.0)
        normal = [base[:, col(q)] for q in range(3)]
        pressure = (normal[0] + normal[1] + normal[2]) / 3.0
        for q in range(3):
            state[:, col(q)] = pressure + factor * (normal[q] - pressure)
        for q in range(3, 6):
            state[:, col(q)] = factor * base[:, col(q)]
        for q in range(6, quant):
            state[:, col(q)] = base[:, col(q)]
        for position in range(4):

            @pl.when(exists(position))
            def _():
                copy_of(step, position).wait_send()

    state[...] = dofs_ref[...]
    turned[...] = jnp.zeros(turned.shape, F32)
    recv_zero = jnp.zeros((seg, 4 * slots), F32)
    for position in range(4):

        @pl.when(jnp.logical_not(exists(position)))
        def _():
            for step in range(RATE):
                recv[step, position] = recv_zero

    def first_emit(term, q, value):
        for s in range(RATE):
            part = weight_ref[s, term] * value
            if isinstance(term, int) and term == 0:
                pieces[s, :, col(q)] = part
            else:
                pieces[s, :, col(q)] += part

    series(first_emit)
    exchange(0, True, False)

    def substep(step, carry):
        def emit(term, q, value):
            part = weight_ref[0, term] * value
            if isinstance(term, int) and term == 0:
                pred[:, col(q)] = part
            else:
                pred[:, col(q)] += part

        series(emit)
        for q in range(quant):
            pred[:, col(q)] = jnp.where(fine, pred[:, col(q)], pieces[step, :, col(q)])
        exchange(step, False, step == RATE - 1)
        return carry

    lax.fori_loop(1, RATE, substep, 0)
    out_ref[...] = state[...]


def shards(
    devices,
    dofs,
    star,
    flux_minus,
    flux_plus,
    cohesion,
    stiff,
    face_proj,
    lift,
    rotate,
    cluster,
    neighbor,
    neigh_face,
    orient,
    send_elem,
    send_face,
):
    basis, quant, elems = dofs.shape
    faces, fbasis, _ = face_proj.shape
    slots = send_elem.shape[1]
    fpad = round_up(fbasis, 8)
    bpad = round_up(basis, 16)
    frows = faces * fpad
    rows = 3 * basis
    skew = 0.5 * (stiff - jnp.transpose(stiff, (0, 2, 1)))
    proj = jnp.pad(face_proj, ((0, 0), (0, fpad - fbasis), (0, 0)))
    main = jnp.concatenate([-skew.reshape(rows, basis), proj.reshape(frows, basis)], axis=0)
    main = jnp.pad(main, ((0, round_up(rows + frows, 16) - rows - frows), (0, bpad - basis)))
    main = jnp.tile(main, (1, 3))
    spun = jnp.einsum("kij,fjb->kfib", rotate, face_proj, precision=lax.Precision.HIGHEST)
    spun = jnp.pad(spun, ((0, 0), (0, 0), (0, fpad - fbasis), (0, bpad - basis)))
    spun = jnp.tile(spun.reshape(3 * frows, bpad), (1, 3))
    left = jnp.pad(jnp.transpose(lift, (1, 0, 2)), ((0, bpad - basis), (0, 0), (0, fpad - fbasis)))
    left = jnp.tile(left.reshape(bpad, frows), (1, 2))
    slot = (send_face * elems + send_elem).reshape(1, -1)
    weights = np.array(
        [interval_weights(s / RATE, (s + 1) / RATE) for s in range(RATE)], np.float32
    )
    dims = (basis, quant, elems, fpad, faces, slots)
    flat = quant * elems
    gathered = 4 * basis
    vmem = pl.BlockSpec(memory_space=pltpu.VMEM)
    scratch = [
        pltpu.VMEM(star.shape, F32),
        pltpu.VMEM(main.shape, BF16),
        pltpu.VMEM(spun.shape, BF16),
        pltpu.VMEM(left.shape, BF16),
        pltpu.VMEM((bpad, frows), BF16),
        pltpu.VMEM((faces * elems, faces * elems), BF16),
        pltpu.VMEM((4 * slots, faces * elems), BF16),
        pltpu.VMEM((faces * elems, 4 * slots), BF16),
        pltpu.VMEM((basis, flat), F32),
        pltpu.VMEM((RATE, basis, flat), F32),
        pltpu.VMEM((basis, flat), F32),
        pltpu.VMEM((3 * bpad, flat), BF16),
        pltpu.VMEM((rows, flat), F32),
        pltpu.VMEM((rows, flat), F32),
        pltpu.VMEM((frows, flat), F32),
        pltpu.VMEM((gathered, faces * elems), F32),
        pltpu.VMEM((gathered, faces * elems), F32),
        pltpu.VMEM((frows, flat), F32),
        pltpu.VMEM((basis, flat), F32),
        pltpu.VMEM((RATE, 4, basis, 4 * slots), F32),
        pltpu.VMEM((RATE, 4, basis, 4 * slots), F32),
        pltpu.SemaphoreType.DMA((RATE, 4)),
        pltpu.SemaphoreType.DMA((RATE, 4)),
    ]
    result = pl.pallas_call(
        functools.partial(kernel, devices, dims),
        out_shape=jax.ShapeDtypeStruct((basis, flat), F32),
        in_specs=[pl.BlockSpec(memory_space=pltpu.SMEM)] + [vmem] * 13,
        out_specs=vmem,
        scratch_shapes=scratch,
        compiler_params=pltpu.CompilerParams(
            collective_id=0, has_side_effects=True, vmem_limit_bytes=40 * 1024 * 1024
        ),
    )(
        jnp.asarray(weights),
        dofs.reshape(basis, flat),
        star,
        flux_minus,
        flux_plus,
        cohesion.reshape(1, elems),
        cluster.reshape(1, elems),
        neighbor,
        neigh_face,
        orient,
        slot,
        main,
        spun,
        left,
    )
    return result.reshape(basis, quant, elems)


def solution(mesh):
    placed = (
        P(None, None, "dom"),
        P(None, None, None, "dom"),
        P(None, None, None, "dom"),
        P(None, None, None, "dom"),
        P("dom"),
        P(),
        P(),
        P(),
        P(),
        P("dom"),
        P(None, "dom"),
        P(None, "dom"),
        P(None, "dom"),
        P(None, "dom"),
        P(None, "dom"),
    )
    return jax.shard_map(
        functools.partial(shards, mesh.shape["dom"]),
        mesh=mesh,
        in_specs=placed,
        out_specs=P(None, None, "dom"),
        check_vma=False,
    )
```

```python
import functools
import math

import jax
import jax.numpy as jnp
import numpy as np
from jax import lax
from jax.experimental import pallas as pl
from jax.experimental.pallas import tpu as pltpu
from jax.sharding import PartitionSpec as P

ORDER = 6
RATE = 4
OFFSETS = (-2, -1, 1, 2)
F32 = jnp.float32
BF16 = jnp.bfloat16


def round_up(value, multiple):
    return -(-value // multiple) * multiple


def interval_weights(begin_time, end_time):
    return [
        (end_time ** (term + 1) - begin_time ** (term + 1)) / math.factorial(term + 1)
        for term in range(ORDER)
    ]


def high(values):
    return values.astype(BF16).astype(F32)


def mm(left, right):
    return jnp.dot(left, right, preferred_element_type=F32)


def kernel(
    devices,
    dims,
    weight_ref,
    *refs,
):
    sources, rest = refs[:15], refs[15:]
    out_ref, rest = rest[0], rest[1:]
    loaded, rest = rest[:15], rest[15:]
    kernel_body(devices, dims, weight_ref, sources, out_ref, loaded, *rest)


def kernel_body(
    devices,
    dims,
    weight_ref,
    sources,
    out_ref,
    loaded,
    load_sem,
    sym_ref,
    main_ref,
    turned_ref,
    lift_high,
    lift_low,
    onehot_local,
    onehot_ghost,
    onehot_send,
    state,
    pieces,
    pred,
    rhs,
    ya,
    yb,
    own_trace,
    turned,
    remote,
    flux,
    base,
    send,
    recv,
    send_sem,
    recv_sem,
):
    basis, quant, elems, fbasis, faces, slots = dims
    (
        dofs_ref,
        star_ref,
        minus_ref,
        plus_ref,
        cohesion_ref,
        stiff_ref,
        proj_ref,
        lift_ref,
        rotate_ref,
        fine_ref,
        neighbor_ref,
        face_ref,
        orient_ref,
        send_elem_ref,
        send_face_ref,
    ) = loaded
    loads = [
        pltpu.make_async_copy(source, target, load_sem.at[i])
        for i, (source, target) in enumerate(zip(sources, loaded))
    ]
    for load in loads:
        load.start()
    fpad = round_up(fbasis, 8)
    bpad = round_up(basis, 16)
    rows = 3 * basis
    groups = [range(q, min(q + 4, quant)) for q in range(0, quant, 4)]
    frows = faces * fpad
    trows = quant * fpad
    seg = basis
    me = lax.axis_index("dom")

    def exists(position):
        other = me + OFFSETS[position]
        return (other >= 0) & (other < devices)

    barrier = pltpu.get_barrier_semaphore()
    for position in range(4):

        @pl.when(exists(position))
        def _():
            pl.semaphore_signal(
                barrier,
                inc=1,
                device_id=(me + OFFSETS[position],),
                device_id_type=pl.DeviceIdType.MESH,
            )

    def col(q):
        return slice(q * elems, (q + 1) * elems)

    def gcol(group):
        return slice(group[0] * elems, (group[-1] + 1) * elems)

    for load in loads:
        load.wait()

    for c in range(3):
        for q in range(quant):
            for p in range(q, quant):
                both = 0.5 * (star_ref[q, p, c : c + 1, :] + star_ref[p, q, c : c + 1, :])
                sym_ref[c, q, p : p + 1, :] = both
                if p != q:
                    sym_ref[c, p, q : q + 1, :] = both

    def spread(matrix, width, offsets):
        height, count = matrix.shape
        row = lax.broadcasted_iota(jnp.int32, (count, width), 0)
        lane = lax.broadcasted_iota(jnp.int32, (count, width), 1)
        hit = lane == row + offsets[0]
        for offset in offsets[1:]:
            hit = hit | (lane == row + offset)
        place = jnp.where(hit, 1.0, 0.0).astype(BF16)
        top = high(matrix)
        return mm(top.astype(BF16), place), mm((matrix - top).astype(BF16), place)

    def left_side(matrix):
        upper, lower = spread(matrix, 3 * bpad, (0, bpad, 2 * bpad))
        lane = lax.broadcasted_iota(jnp.int32, upper.shape, 1)
        return jnp.where(lane < 2 * bpad, upper, lower)

    def pad_rows(matrix, count):
        if count == matrix.shape[0]:
            return matrix
        blank = jnp.zeros((count - matrix.shape[0], matrix.shape[1]), F32)
        return jnp.concatenate([matrix, blank], axis=0)

    projections = [pad_rows(proj_ref[:, f, :], fpad) for f in range(faces)]
    blocks = []
    for c in range(3):
        whole = stiff_ref[c]
        blocks.append(0.5 * (jnp.transpose(whole) - whole))
    blocks = jnp.concatenate(blocks + projections, axis=0)
    main_ref[...] = left_side(pad_rows(blocks, main_ref.shape[0])).astype(BF16)
    for k in range(3):
        spun = [
            pad_rows(
                jnp.dot(
                    rotate_ref[k],
                    proj_ref[:, f, :],
                    preferred_element_type=F32,
                    precision=lax.Precision.HIGHEST,
                ),
                fpad,
            )
            for f in range(faces)
        ]
        turned_ref[k * frows : (k + 1) * frows, :] = left_side(
            jnp.concatenate(spun, axis=0)
        ).astype(BF16)
    upper, lower = None, None
    for f in range(faces):
        one, two = spread(
            pad_rows(jnp.transpose(pad_rows(lift_ref[:, f, :], fpad)), bpad),
            2 * frows,
            (f * fpad, frows + f * fpad),
        )
        upper = one if upper is None else upper + one
        lower = two if lower is None else lower + two
    lift_high[...] = upper.astype(BF16)
    lift_low[...] = lower[:, 0:frows].astype(BF16)

    def onehot(row_count, index):
        ids = lax.broadcasted_iota(jnp.int32, (row_count, index.shape[1]), 0)
        return jnp.where(ids == index, 1.0, 0.0).astype(BF16)

    for f in range(faces):
        target = neighbor_ref[f : f + 1, :]
        across = face_ref[f : f + 1, :]
        local = jnp.where(target < elems, across * elems + target, -1)
        onehot_local[:, f * elems : (f + 1) * elems] = onehot(faces * elems, local)
        onehot_ghost[:, f * elems : (f + 1) * elems] = onehot(4 * slots, target - elems)
    slot_row = lax.broadcasted_iota(jnp.int32, (slots, 4 * slots), 0)
    slot_lane = lax.broadcasted_iota(jnp.int32, (slots, 4 * slots), 1)
    place = jnp.where(slot_lane % slots == slot_row, 1.0, 0.0).astype(BF16)
    block_row = lax.broadcasted_iota(jnp.int32, (4, 4 * slots), 0)
    block_lane = lax.broadcasted_iota(jnp.int32, (4, 4 * slots), 1) // slots

    def one_row(ref):
        wide = mm(ref[...].astype(F32).astype(BF16), place)
        return jnp.sum(jnp.where(block_lane == block_row, wide, 0.0), axis=0, keepdims=True)

    slot = one_row(send_face_ref) * elems + one_row(send_elem_ref)
    onehot_send[...] = onehot(faces * elems, slot.astype(jnp.int32))

    fine = fine_ref[...] == 1

    def put(q, values):
        top = high(values)
        pad = jnp.zeros((bpad - basis, elems), F32)
        upper = jnp.concatenate([values, pad], axis=0).astype(BF16)
        lower = jnp.concatenate([values - top, pad], axis=0).astype(BF16)
        rhs[0:bpad, col(q)] = upper
        rhs[bpad : 2 * bpad, col(q)] = lower
        rhs[2 * bpad : 3 * bpad, col(q)] = upper

    skew_rows = round_up(rows, 16)

    def product(group, target):
        result = mm(main_ref[0:skew_rows, :], rhs[:, gcol(group)])
        target[:, gcol(group)] = result[0:rows]

    def stage(source, target, emit):
        for group in groups:
            sums = [None] * len(group)
            for c in range(3):
                for p in range(quant):
                    values = source[c * basis : (c + 1) * basis, col(p)]
                    for i, q in enumerate(group):
                        term = sym_ref[c, q, p : p + 1, :] * values
                        sums[i] = term if sums[i] is None else sums[i] + term
            for i, q in enumerate(group):
                emit(q, sums[i])
                if target is not None:
                    put(q, sums[i])
            if target is not None:
                product(group, target)

    def series(emit):
        for group in groups:
            for i, q in enumerate(group):
                emit(0, q, state[:, col(q)])
                put(q, state[:, col(q)])
            product(group, ya)

        def pair(j, carry):
            stage(ya, yb, functools.partial(emit, 2 * j + 1))
            stage(yb, ya, functools.partial(emit, 2 * j + 2))
            return carry

        lax.fori_loop(0, 2, pair, 0)
        stage(ya, None, functools.partial(emit, 5))

    def copy_of(step, position):
        return pltpu.make_async_remote_copy(
            src_ref=send.at[step, position],
            dst_ref=recv.at[step, 3 - position],
            send_sem=send_sem.at[step, position],
            recv_sem=recv_sem.at[step, 3 - position],
            device_id=(me + OFFSETS[position],),
            device_id_type=pl.DeviceIdType.MESH,
        )

    lane_seg = lax.broadcasted_iota(jnp.int32, (seg, 4 * slots), 1) // slots

    def repack(parts):
        made = []
        for b in range(4):
            value = parts[0] if b == 0 else pltpu.roll(parts[0], (4 - b) * slots, 1)
            for j in range(1, 4):
                shift = ((j - b) % 4) * slots
                moved = parts[j] if shift == 0 else pltpu.roll(parts[j], shift, 1)
                value = jnp.where(lane_seg == j, moved, value)
            made.append(value)
        return made

    def two_halves(values):
        top = high(values)
        return top.astype(BF16), (values - top).astype(BF16)

    def exchange(step, first, last):
        for group in groups:
            for i, q in enumerate(group):
                put(q, pieces[0, :, col(q)] if first else pred[:, col(q)])
            result = mm(turned_ref[...], rhs[:, gcol(group)])
            for i, q in enumerate(group):
                for f in range(faces):
                    code = orient_ref[f : f + 1, :]
                    options = [
                        result[
                            k * frows + f * fpad : k * frows + (f + 1) * fpad,
                            i * elems : (i + 1) * elems,
                        ]
                        for k in range(3)
                    ]
                    turned[q * fpad : (q + 1) * fpad, f * elems : (f + 1) * elems] = jnp.where(
                        code == 0, options[0], jnp.where(code == 1, options[2], options[1])
                    )
        top, low = two_halves(turned[...])
        sending = mm(top, onehot_send[...]) + mm(low, onehot_send[...])
        parts = [sending[j * seg : (j + 1) * seg] for j in range(4)]
        for b, value in enumerate(repack(parts)):
            send[step, b] = value
        if first:
            peers = sum(exists(position).astype(jnp.int32) for position in range(4))
            pl.semaphore_wait(barrier, peers)
        for position in range(4):

            @pl.when(exists(position))
            def _():
                copy_of(step, position).start()

        remote[...] = mm(top, onehot_local[...]) + mm(low, onehot_local[...])
        if first:
            for q in range(quant):
                whole = pieces[0, :, col(q)]
                for other in range(1, RATE):
                    whole = whole + pieces[other, :, col(q)]
                put(q, jnp.where(fine, pieces[0, :, col(q)], whole))
        for group in groups:
            result = mm(main_ref[...], rhs[:, gcol(group)])
            ya[:, gcol(group)] = result[0:rows]
            own_trace[:, gcol(group)] = result[rows : rows + frows]

        def volume(q, value):
            if not first:
                value = jnp.where(fine, value, 0.0)
            base[:, col(q)] = state[:, col(q)] + value

        stage(ya, None, volume)

        def solver(matrix_ref, f, group, load):
            sums = [None] * len(group)
            for p in range(quant):
                values = load(p)
                for i, q in enumerate(group):
                    term = matrix_ref[q, p, f : f + 1, :] * values
                    sums[i] = term if sums[i] is None else sums[i] + term
            return sums

        for f in range(faces):
            frange = slice(f * fpad, (f + 1) * fpad)
            for group in groups:
                sums = solver(minus_ref, f, group, lambda p: own_trace[frange, col(p)])
                for i, q in enumerate(group):
                    value = sums[i] if first else jnp.where(fine, sums[i], 0.0)
                    flux[frange, col(q)] = value
        for position in range(4):

            @pl.when(exists(position))
            def _():
                copy_of(step, 3 - position).wait_recv()

        ghosts = repack([recv[step, b] for b in range(4)])
        ghost = jnp.concatenate(ghosts, axis=0)
        top, low = two_halves(ghost)
        remote[...] += mm(top, onehot_ghost[...]) + mm(low, onehot_ghost[...])
        for f in range(faces):
            frange = slice(f * fpad, (f + 1) * fpad)
            for group in groups:
                sums = solver(
                    plus_ref,
                    f,
                    group,
                    lambda p: remote[p * fpad : (p + 1) * fpad, f * elems : (f + 1) * elems],
                )
                for i, q in enumerate(group):
                    flux[frange, col(q)] += sums[i]
        for group in groups:
            top, low = two_halves(flux[:, gcol(group)])
            lifted = mm(lift_high[...], jnp.concatenate([top, low], axis=0)) + mm(
                lift_low[...], top
            )
            base[:, gcol(group)] = base[:, gcol(group)] - lifted[0:basis]
        s = [base[0:1, col(q)] for q in range(6)]
        mean = (s[0] + s[1] + s[2]) / 3.0
        d = [s[i] - mean for i in range(3)]
        second = (
            0.5 * (d[0] * d[0] + d[1] * d[1] + d[2] * d[2])
            + s[3] * s[3]
            + s[4] * s[4]
            + s[5] * s[5]
        )
        cohesion = cohesion_ref[...]
        factor = cohesion / jnp.maximum(jnp.sqrt(second), cohesion)
        if last is not True:
            factor = jnp.where(fine | last, factor, 1.0)
        normal = [base[:, col(q)] for q in range(3)]
        pressure = (normal[0] + normal[1] + normal[2]) / 3.0
        for q in range(3):
            state[:, col(q)] = pressure + factor * (normal[q] - pressure)
        for q in range(3, 6):
            state[:, col(q)] = factor * base[:, col(q)]
        for q in range(6, quant):
            state[:, col(q)] = base[:, col(q)]
        for position in range(4):

            @pl.when(exists(position))
            def _():
                copy_of(step, position).wait_send()

    for q in range(quant):
        state[:, col(q)] = dofs_ref[q]
    turned[...] = jnp.zeros(turned.shape, F32)
    recv_zero = jnp.zeros((seg, 4 * slots), F32)
    for position in range(4):

        @pl.when(jnp.logical_not(exists(position)))
        def _():
            for step in range(RATE):
                recv[step, position] = recv_zero

    def first_emit(term, q, value):
        for s in range(RATE):
            part = weight_ref[s, term] * value
            if isinstance(term, int) and term == 0:
                pieces[s, :, col(q)] = part
            else:
                pieces[s, :, col(q)] += part

    series(first_emit)
    exchange(0, True, False)

    def substep(step, carry):
        def emit(term, q, value):
            part = weight_ref[0, term] * value
            if isinstance(term, int) and term == 0:
                pred[:, col(q)] = part
            else:
                pred[:, col(q)] += part

        series(emit)
        for q in range(quant):
            pred[:, col(q)] = jnp.where(fine, pred[:, col(q)], pieces[step, :, col(q)])
        exchange(step, False, step == RATE - 1)
        return carry

    lax.fori_loop(1, RATE, substep, 0)
    for q in range(quant):
        out_ref[q] = state[:, col(q)]


def shards(
    devices,
    dofs,
    star,
    flux_minus,
    flux_plus,
    cohesion,
    stiff,
    face_proj,
    lift,
    rotate,
    cluster,
    neighbor,
    neigh_face,
    orient,
    send_elem,
    send_face,
):
    basis, quant, elems = dofs.shape
    faces, fbasis, _ = face_proj.shape
    slots = send_elem.shape[1]
    fpad = round_up(fbasis, 8)
    bpad = round_up(basis, 16)
    frows = faces * fpad
    rows = 3 * basis
    weights = np.array(
        [interval_weights(s / RATE, (s + 1) / RATE) for s in range(RATE)], np.float32
    )
    dims = (basis, quant, elems, fbasis, faces, slots)
    flat = quant * elems
    gathered = 4 * basis
    vmem = pl.BlockSpec(memory_space=pltpu.VMEM)
    arrays = [
        jnp.transpose(dofs, (1, 0, 2)),
        jnp.transpose(star, (1, 2, 0, 3)),
        jnp.transpose(flux_minus, (1, 2, 0, 3)),
        jnp.transpose(flux_plus, (1, 2, 0, 3)),
        cohesion.reshape(1, elems),
        stiff,
        jnp.transpose(face_proj, (1, 0, 2)),
        jnp.transpose(lift, (2, 0, 1)),
        rotate,
        cluster.reshape(1, elems),
        neighbor,
        neigh_face,
        orient,
        send_elem,
        send_face,
    ]
    scratch = [pltpu.VMEM(array.shape, array.dtype) for array in arrays] + [
        pltpu.SemaphoreType.DMA((len(arrays),)),
        pltpu.VMEM(star.shape, F32),
        pltpu.VMEM((round_up(rows + frows, 16), 3 * bpad), BF16),
        pltpu.VMEM((3 * frows, 3 * bpad), BF16),
        pltpu.VMEM((bpad, 2 * frows), BF16),
        pltpu.VMEM((bpad, frows), BF16),
        pltpu.VMEM((faces * elems, faces * elems), BF16),
        pltpu.VMEM((4 * slots, faces * elems), BF16),
        pltpu.VMEM((faces * elems, 4 * slots), BF16),
        pltpu.VMEM((basis, flat), F32),
        pltpu.VMEM((RATE, basis, flat), F32),
        pltpu.VMEM((basis, flat), F32),
        pltpu.VMEM((3 * bpad, flat), BF16),
        pltpu.VMEM((rows, flat), F32),
        pltpu.VMEM((rows, flat), F32),
        pltpu.VMEM((frows, flat), F32),
        pltpu.VMEM((gathered, faces * elems), F32),
        pltpu.VMEM((gathered, faces * elems), F32),
        pltpu.VMEM((frows, flat), F32),
        pltpu.VMEM((basis, flat), F32),
        pltpu.VMEM((RATE, 4, basis, 4 * slots), F32),
        pltpu.VMEM((RATE, 4, basis, 4 * slots), F32),
        pltpu.SemaphoreType.DMA((RATE, 4)),
        pltpu.SemaphoreType.DMA((RATE, 4)),
    ]
    result = pl.pallas_call(
        functools.partial(kernel, devices, dims),
        out_shape=jax.ShapeDtypeStruct((quant, basis, elems), F32),
        in_specs=[pl.BlockSpec(memory_space=pltpu.SMEM)] + [pl.BlockSpec(memory_space=pl.ANY)] * len(arrays),
        out_specs=vmem,
        scratch_shapes=scratch,
        compiler_params=pltpu.CompilerParams(
            collective_id=0, has_side_effects=True, vmem_limit_bytes=60 * 1024 * 1024
        ),
    )(
        jnp.asarray(weights),
        *arrays,
    )
    return jnp.transpose(result, (1, 0, 2))


def solution(mesh):
    placed = (
        P(None, None, "dom"),
        P(None, None, None, "dom"),
        P(None, None, None, "dom"),
        P(None, None, None, "dom"),
        P("dom"),
        P(),
        P(),
        P(),
        P(),
        P("dom"),
        P(None, "dom"),
        P(None, "dom"),
        P(None, "dom"),
        P(None, "dom"),
        P(None, "dom"),
    )
    return jax.shard_map(
        functools.partial(shards, mesh.shape["dom"]),
        mesh=mesh,
        in_specs=placed,
        out_specs=P(None, None, "dom"),
        check_vma=False,
    )
```

```python
import functools
import math

import jax
import jax.numpy as jnp
import numpy as np
from jax import lax
from jax.experimental import pallas as pl
from jax.experimental.pallas import tpu as pltpu
from jax.sharding import PartitionSpec as P

ORDER = 6
RATE = 4
OFFSETS = (-2, -1, 1, 2)
F32 = jnp.float32
BF16 = jnp.bfloat16


def round_up(value, multiple):
    return -(-value // multiple) * multiple


def interval_weights(begin_time, end_time):
    return [
        (end_time ** (term + 1) - begin_time ** (term + 1)) / math.factorial(term + 1)
        for term in range(ORDER)
    ]


def high(values):
    return values.astype(BF16).astype(F32)


def mm(left, right):
    return jnp.dot(left, right, preferred_element_type=F32)


def kernel(
    devices,
    dims,
    weight_ref,
    *refs,
):
    sources, rest = refs[:15], refs[15:]
    out_ref, rest = rest[0], rest[1:]
    loaded, rest = rest[:15], rest[15:]
    kernel_body(devices, dims, weight_ref, sources, out_ref, loaded, *rest)


def kernel_body(
    devices,
    dims,
    weight_ref,
    sources,
    out_ref,
    loaded,
    load_sem,
    sym_ref,
    sym_roll,
    sym_pack,
    minus_flat,
    minus_pack,
    plus_flat,
    acc,
    main_ref,
    turned_ref,
    lift_high,
    lift_low,
    onehot_local,
    onehot_ghost,
    onehot_send,
    state,
    pieces,
    pred,
    rhs,
    ya,
    yb,
    own_trace,
    turned,
    remote,
    flux,
    base,
    send,
    recv,
    send_sem,
    recv_sem,
):
    basis, quant, elems, fbasis, faces, slots = dims
    (
        dofs_ref,
        star_ref,
        minus_ref,
        plus_ref,
        cohesion_ref,
        stiff_ref,
        proj_ref,
        lift_ref,
        rotate_ref,
        fine_ref,
        neighbor_ref,
        face_ref,
        orient_ref,
        send_elem_ref,
        send_face_ref,
    ) = loaded
    loads = [
        pltpu.make_async_copy(source, target, load_sem.at[i])
        for i, (source, target) in enumerate(zip(sources, loaded))
    ]
    for load in loads:
        load.start()
    fpad = round_up(fbasis, 8)
    bpad = round_up(basis, 16)
    rows = 3 * basis
    groups = [range(q, min(q + 4, quant)) for q in range(0, quant, 4)]
    frows = faces * fpad
    trows = quant * fpad
    seg = basis
    me = lax.axis_index("dom")

    def exists(position):
        other = me + OFFSETS[position]
        return (other >= 0) & (other < devices)

    barrier = pltpu.get_barrier_semaphore()
    for position in range(4):

        @pl.when(exists(position))
        def _():
            pl.semaphore_signal(
                barrier,
                inc=1,
                device_id=(me + OFFSETS[position],),
                device_id_type=pl.DeviceIdType.MESH,
            )

    def col(q):
        return slice(q * elems, (q + 1) * elems)

    def gcol(group):
        return slice(group[0] * elems, (group[-1] + 1) * elems)

    for load in loads:
        load.wait()

    half = elems // 2
    lane_id = lax.broadcasted_iota(jnp.int32, (1, elems), 1)
    left_half = lane_id < half
    row_id = lax.broadcasted_iota(jnp.int32, (elems, elems), 0)
    col_id = lax.broadcasted_iota(jnp.int32, (elems, elems), 1)
    is_fine = jnp.where(fine_ref[...] == 1, 1.0, 0.0)
    below = jnp.where(row_id <= col_id, 1.0, 0.0).astype(BF16)
    count = mm(jnp.broadcast_to(is_fine, (16, elems)).astype(BF16), below)[0:1]
    total = jnp.sum(is_fine, axis=1, keepdims=True)
    lane_f = lane_id.astype(F32)
    place_of = jnp.where(is_fine > 0.5, count - 1.0, total + lane_f - count)
    back_f = jnp.where(row_id.astype(F32) == place_of, 1.0, 0.0)
    back = back_f.astype(BF16)
    order = jnp.transpose(back_f).astype(BF16)
    fine = lane_f < total

    def permute(values, matrix):
        top = high(values)
        return mm(top.astype(BF16), matrix) + mm((values - top).astype(BF16), matrix)

    def swap(values):
        return pltpu.roll(values, half, 1)

    for c in range(3):
        for q in range(quant):
            for p in range(q, quant):
                both = 0.5 * (star_ref[q, p, c : c + 1, :] + star_ref[p, q, c : c + 1, :])
                at = (c * quant + q) * quant + p
                sym_ref[at : at + 1, :] = both
                if p != q:
                    at = (c * quant + p) * quant + q
                    sym_ref[at : at + 1, :] = both
    for q in range(quant):
        for p in range(quant):
            at = (q * quant + p) * faces
            minus_flat[at : at + faces, :] = minus_ref[q, p]
            plus_flat[at : at + faces, :] = plus_ref[q, p]
    sym_ref[...] = permute(sym_ref[...], order)
    sym_roll[...] = swap(sym_ref[...])
    minus_flat[...] = permute(minus_flat[...], order)
    plus_flat[...] = permute(plus_flat[...], order)

    def sym_at(c, q, p):
        at = (c * quant + q) * quant + p
        return slice(at, at + 1)

    last_q = quant - 1
    for q in range(quant):
        for c in range(3):
            for t in range(4):
                at = q * 14 + c * 4 + t
                sym_pack[at : at + 1, :] = jnp.where(
                    left_half, sym_ref[sym_at(c, q, 2 * t), :], sym_roll[sym_at(c, q, 2 * t + 1), :]
                )
        at = q * 14 + 12
        sym_pack[at : at + 1, :] = jnp.where(
            left_half, sym_ref[sym_at(0, q, last_q), :], sym_roll[sym_at(1, q, last_q), :]
        )
        sym_pack[at + 1 : at + 2, :] = jnp.where(left_half, sym_ref[sym_at(2, q, last_q), :], 0.0)
        for f in range(faces):
            for t in range(5):
                at = (q * faces + f) * 5 + t
                one = (q * quant + 2 * t) * faces + f
                two = one + faces
                right = swap(minus_flat[two : two + 1, :]) if t < 4 else 0.0
                minus_pack[at : at + 1, :] = jnp.where(
                    left_half, minus_flat[one : one + 1, :], right
                )

    def spread(matrix, width, offsets):
        height, count = matrix.shape
        row = lax.broadcasted_iota(jnp.int32, (count, width), 0)
        lane = lax.broadcasted_iota(jnp.int32, (count, width), 1)
        hit = lane == row + offsets[0]
        for offset in offsets[1:]:
            hit = hit | (lane == row + offset)
        place = jnp.where(hit, 1.0, 0.0).astype(BF16)
        top = high(matrix)
        return mm(top.astype(BF16), place), mm((matrix - top).astype(BF16), place)

    def left_side(matrix):
        upper, lower = spread(matrix, 3 * bpad, (0, bpad, 2 * bpad))
        lane = lax.broadcasted_iota(jnp.int32, upper.shape, 1)
        return jnp.where(lane < 2 * bpad, upper, lower)

    def pad_rows(matrix, count):
        if count == matrix.shape[0]:
            return matrix
        blank = jnp.zeros((count - matrix.shape[0], matrix.shape[1]), F32)
        return jnp.concatenate([matrix, blank], axis=0)

    projections = [pad_rows(proj_ref[:, f, :], fpad) for f in range(faces)]
    blocks = []
    for c in range(3):
        whole = stiff_ref[c]
        blocks.append(0.5 * (jnp.transpose(whole) - whole))
    blocks = jnp.concatenate(blocks + projections, axis=0)
    main_ref[...] = left_side(pad_rows(blocks, main_ref.shape[0])).astype(BF16)
    for k in range(3):
        spun = [
            pad_rows(
                jnp.dot(
                    rotate_ref[k],
                    proj_ref[:, f, :],
                    preferred_element_type=F32,
                    precision=lax.Precision.HIGHEST,
                ),
                fpad,
            )
            for f in range(faces)
        ]
        turned_ref[k * frows : (k + 1) * frows, :] = left_side(
            jnp.concatenate(spun, axis=0)
        ).astype(BF16)
    upper, lower = None, None
    for f in range(faces):
        one, two = spread(
            pad_rows(jnp.transpose(pad_rows(lift_ref[:, f, :], fpad)), bpad),
            2 * frows,
            (f * fpad, frows + f * fpad),
        )
        upper = one if upper is None else upper + one
        lower = two if lower is None else lower + two
    lift_high[...] = upper.astype(BF16)
    lift_low[...] = lower[:, 0:frows].astype(BF16)

    def onehot(row_count, index):
        ids = lax.broadcasted_iota(jnp.int32, (row_count, index.shape[1]), 0)
        return jnp.where(ids == index, 1.0, 0.0).astype(BF16)

    def permuted_ids(ref):
        return mm(ref[...].astype(F32).astype(BF16), order).astype(jnp.int32)

    neighbor_ids = permuted_ids(neighbor_ref)
    face_ids = permuted_ids(face_ref)
    orient_ids = permuted_ids(orient_ref)

    def sorted_rows(f, raw):
        return mm(back, raw[f * elems : (f + 1) * elems]).astype(BF16)

    for f in range(faces):
        target = neighbor_ids[f : f + 1, :]
        across = face_ids[f : f + 1, :]
        local = jnp.where(target < elems, across * elems + target, -1)
        raw = onehot(faces * elems, local)
        for g in range(faces):
            onehot_local[g * elems : (g + 1) * elems, f * elems : (f + 1) * elems] = sorted_rows(
                g, raw
            )
        onehot_ghost[:, f * elems : (f + 1) * elems] = onehot(4 * slots, target - elems)
    slot_row = lax.broadcasted_iota(jnp.int32, (slots, 4 * slots), 0)
    slot_lane = lax.broadcasted_iota(jnp.int32, (slots, 4 * slots), 1)
    place = jnp.where(slot_lane % slots == slot_row, 1.0, 0.0).astype(BF16)
    block_row = lax.broadcasted_iota(jnp.int32, (4, 4 * slots), 0)
    block_lane = lax.broadcasted_iota(jnp.int32, (4, 4 * slots), 1) // slots

    def one_row(ref):
        wide = mm(ref[...].astype(F32).astype(BF16), place)
        return jnp.sum(jnp.where(block_lane == block_row, wide, 0.0), axis=0, keepdims=True)

    slot = one_row(send_face_ref) * elems + one_row(send_elem_ref)
    raw = onehot(faces * elems, slot.astype(jnp.int32))
    for g in range(faces):
        onehot_send[g * elems : (g + 1) * elems, :] = sorted_rows(g, raw)
    wide_cohesion = jnp.broadcast_to(cohesion_ref[...], (16, elems))
    coh_top = high(wide_cohesion)
    coh_rest = wide_cohesion - coh_top
    coh_mid = high(coh_rest)
    sorted_cohesion = (
        mm(coh_top.astype(BF16), order)
        + mm(coh_mid.astype(BF16), order)
        + mm((coh_rest - coh_mid).astype(BF16), order)
    )[0:1]


    def put(q, values):
        top = high(values)
        pad = jnp.zeros((bpad - basis, elems), F32)
        upper = jnp.concatenate([values, pad], axis=0).astype(BF16)
        lower = jnp.concatenate([values - top, pad], axis=0).astype(BF16)
        rhs[0:bpad, col(q)] = upper
        rhs[bpad : 2 * bpad, col(q)] = lower
        rhs[2 * bpad : 3 * bpad, col(q)] = upper

    skew_rows = round_up(rows, 16)

    def product(group, target):
        result = mm(main_ref[0:skew_rows, :], rhs[:, gcol(group)])
        target[:, gcol(group)] = result[0:rows]

    def stage(source, target, emit):
        for group in groups:
            sums = [None] * len(group)
            for c in range(3):
                for p in range(quant):
                    values = source[c * basis : (c + 1) * basis, col(p)]
                    for i, q in enumerate(group):
                        term = sym_ref[sym_at(c, q, p), :] * values
                        sums[i] = term if sums[i] is None else sums[i] + term
            for i, q in enumerate(group):
                emit(q, sums[i])
                if target is not None:
                    put(q, sums[i])
            if target is not None:
                product(group, target)

    tiles = ((0, 1), (2, 3), (4,))

    def tile_cols(part):
        return slice(tiles[part][0] * elems, (tiles[part][-1] + 1) * elems)

    def packed_product(part, target):
        result = mm(main_ref[0:skew_rows, :], rhs[:, tile_cols(part)])
        target[:, tile_cols(part)] = result[0:rows]

    def pack(t, values):
        if t < 4:
            put(t, jnp.where(left_half, values[0], values[1]))
        else:
            put(t, values[0])

    def packed_stage(source, target, emit):
        for part, group in enumerate(groups):
            sums = [None] * len(group)
            for k in range(14):
                if k < 12:
                    c, t = k // 4, k % 4
                    values = source[c * basis : (c + 1) * basis, col(t)]
                elif k == 12:
                    values = jnp.where(
                        left_half, source[0:basis, col(4)], source[basis : 2 * basis, col(4)]
                    )
                else:
                    values = source[2 * basis : 3 * basis, col(4)]
                for i, q in enumerate(group):
                    term = sym_pack[q * 14 + k : q * 14 + k + 1, :] * values
                    sums[i] = term if sums[i] is None else sums[i] + term
            sums = [value + swap(value) for value in sums]
            for i, q in enumerate(group):
                emit(q, sums[i])
            if target is not None:
                for i, t in enumerate(tiles[part]):
                    pack(t, sums[2 * i : 2 * i + 2])
                packed_product(part, target)

    def packed_series(emit):
        for part, group in enumerate(groups):
            both = []
            for q in group:
                value = state[:, col(q)]
                value = jnp.where(left_half, value, swap(value))
                emit(0, q, value)
                both.append(value)
            for i, t in enumerate(tiles[part]):
                pack(t, both[2 * i : 2 * i + 2])
            packed_product(part, ya)

        def pair(j, carry):
            packed_stage(ya, yb, functools.partial(emit, 2 * j + 1))
            packed_stage(yb, ya, functools.partial(emit, 2 * j + 2))
            return carry

        lax.fori_loop(0, 2, pair, 0)
        packed_stage(ya, None, functools.partial(emit, 5))

    def series(emit):
        for group in groups:
            for i, q in enumerate(group):
                emit(0, q, state[:, col(q)])
                put(q, state[:, col(q)])
            product(group, ya)

        def pair(j, carry):
            stage(ya, yb, functools.partial(emit, 2 * j + 1))
            stage(yb, ya, functools.partial(emit, 2 * j + 2))
            return carry

        lax.fori_loop(0, 2, pair, 0)
        stage(ya, None, functools.partial(emit, 5))

    def copy_of(step, position):
        return pltpu.make_async_remote_copy(
            src_ref=send.at[step, position],
            dst_ref=recv.at[step, 3 - position],
            send_sem=send_sem.at[step, position],
            recv_sem=recv_sem.at[step, 3 - position],
            device_id=(me + OFFSETS[position],),
            device_id_type=pl.DeviceIdType.MESH,
        )

    lane_seg = lax.broadcasted_iota(jnp.int32, (seg, 4 * slots), 1) // slots

    def repack(parts):
        made = []
        for b in range(4):
            value = parts[0] if b == 0 else pltpu.roll(parts[0], (4 - b) * slots, 1)
            for j in range(1, 4):
                shift = ((j - b) % 4) * slots
                moved = parts[j] if shift == 0 else pltpu.roll(parts[j], shift, 1)
                value = jnp.where(lane_seg == j, moved, value)
            made.append(value)
        return made

    def two_halves(values):
        top = high(values)
        return top.astype(BF16), (values - top).astype(BF16)

    def exchange(step, first, last):
        for group in groups:
            for i, q in enumerate(group):
                put(q, pieces[0, :, col(q)] if first else pred[:, col(q)])
            result = mm(turned_ref[...], rhs[:, gcol(group)])
            for i, q in enumerate(group):
                for f in range(faces):
                    code = orient_ids[f : f + 1, :]
                    options = [
                        result[
                            k * frows + f * fpad : k * frows + (f + 1) * fpad,
                            i * elems : (i + 1) * elems,
                        ]
                        for k in range(3)
                    ]
                    turned[q * fpad : (q + 1) * fpad, f * elems : (f + 1) * elems] = jnp.where(
                        code == 0, options[0], jnp.where(code == 1, options[2], options[1])
                    )
        top, low = two_halves(turned[...])
        sending = mm(top, onehot_send[...]) + mm(low, onehot_send[...])
        parts = [sending[j * seg : (j + 1) * seg] for j in range(4)]
        for b, value in enumerate(repack(parts)):
            send[step, b] = value
        if first:
            peers = sum(exists(position).astype(jnp.int32) for position in range(4))
            pl.semaphore_wait(barrier, peers)
        for position in range(4):

            @pl.when(exists(position))
            def _():
                copy_of(step, position).start()

        remote[...] = mm(top, onehot_local[...]) + mm(low, onehot_local[...])
        if first:
            for q in range(quant):
                whole = pieces[0, :, col(q)]
                for other in range(1, RATE):
                    whole = whole + pieces[other, :, col(q)]
                put(q, jnp.where(fine, pieces[0, :, col(q)], whole))
        else:
            for part, group in enumerate(groups):
                for i, t in enumerate(tiles[part]):
                    pack(t, [acc[:, col(q)] for q in group[2 * i : 2 * i + 2]])
        for part, group in enumerate(groups):
            lanes = gcol(group) if first else tile_cols(part)
            result = mm(main_ref[...], rhs[:, lanes])
            ya[:, lanes] = result[0:rows]
            own_trace[:, lanes] = result[rows : rows + frows]

        def volume(q, value):
            if not first:
                value = jnp.where(fine, value, 0.0)
            base[:, col(q)] = state[:, col(q)] + value

        if first:
            stage(ya, None, volume)
        else:
            packed_stage(ya, None, volume)

        def solver(matrix_ref, f, group, load):
            sums = [None] * len(group)
            for p in range(quant):
                values = load(p)
                for i, q in enumerate(group):
                    at = (q * quant + p) * faces + f
                    term = matrix_ref[at : at + 1, :] * values
                    sums[i] = term if sums[i] is None else sums[i] + term
            return sums

        def packed_solver(f, group):
            sums = [None] * len(group)
            for t in range(5):
                values = own_trace[f * fpad : (f + 1) * fpad, col(t)]
                for i, q in enumerate(group):
                    at = (q * faces + f) * 5 + t
                    term = minus_pack[at : at + 1, :] * values
                    sums[i] = term if sums[i] is None else sums[i] + term
            return [jnp.where(fine, value + swap(value), 0.0) for value in sums]

        for f in range(faces):
            frange = slice(f * fpad, (f + 1) * fpad)
            for group in groups:
                if first:
                    sums = solver(minus_flat, f, group, lambda p: own_trace[frange, col(p)])
                else:
                    sums = packed_solver(f, group)
                for i, q in enumerate(group):
                    flux[frange, col(q)] = sums[i]
        for position in range(4):

            @pl.when(exists(position))
            def _():
                copy_of(step, 3 - position).wait_recv()

        ghosts = repack([recv[step, b] for b in range(4)])
        ghost = jnp.concatenate(ghosts, axis=0)
        top, low = two_halves(ghost)
        remote[...] += mm(top, onehot_ghost[...]) + mm(low, onehot_ghost[...])
        for f in range(faces):
            frange = slice(f * fpad, (f + 1) * fpad)
            for group in groups:
                sums = solver(
                    plus_flat,
                    f,
                    group,
                    lambda p: remote[p * fpad : (p + 1) * fpad, f * elems : (f + 1) * elems],
                )
                for i, q in enumerate(group):
                    flux[frange, col(q)] += sums[i]
        for group in groups:
            top, low = two_halves(flux[:, gcol(group)])
            lifted = mm(lift_high[...], jnp.concatenate([top, low], axis=0)) + mm(
                lift_low[...], top
            )
            base[:, gcol(group)] = base[:, gcol(group)] - lifted[0:basis]
        s = [base[0:1, col(q)] for q in range(6)]
        mean = (s[0] + s[1] + s[2]) / 3.0
        d = [s[i] - mean for i in range(3)]
        second = (
            0.5 * (d[0] * d[0] + d[1] * d[1] + d[2] * d[2])
            + s[3] * s[3]
            + s[4] * s[4]
            + s[5] * s[5]
        )
        cohesion = sorted_cohesion
        factor = cohesion / jnp.maximum(jnp.sqrt(second), cohesion)
        if last is not True:
            factor = jnp.where(fine | last, factor, 1.0)
        normal = [base[:, col(q)] for q in range(3)]
        pressure = (normal[0] + normal[1] + normal[2]) / 3.0
        for q in range(3):
            state[:, col(q)] = pressure + factor * (normal[q] - pressure)
        for q in range(3, 6):
            state[:, col(q)] = factor * base[:, col(q)]
        for q in range(6, quant):
            state[:, col(q)] = base[:, col(q)]
        for position in range(4):

            @pl.when(exists(position))
            def _():
                copy_of(step, position).wait_send()

    for q in range(quant):
        state[:, col(q)] = permute(dofs_ref[q], order)
    turned[...] = jnp.zeros(turned.shape, F32)
    recv_zero = jnp.zeros((seg, 4 * slots), F32)
    for position in range(4):

        @pl.when(jnp.logical_not(exists(position)))
        def _():
            for step in range(RATE):
                recv[step, position] = recv_zero

    def first_emit(term, q, value):
        for s in range(RATE):
            part = weight_ref[s, term] * value
            if isinstance(term, int) and term == 0:
                pieces[s, :, col(q)] = part
            else:
                pieces[s, :, col(q)] += part

    series(first_emit)
    exchange(0, True, False)

    def substep(step, carry):
        def emit(term, q, value):
            part = weight_ref[0, term] * value
            if isinstance(term, int) and term == 0:
                acc[:, col(q)] = part
            else:
                acc[:, col(q)] += part

        packed_series(emit)
        for q in range(quant):
            pred[:, col(q)] = jnp.where(fine, acc[:, col(q)], pieces[step, :, col(q)])
        exchange(step, False, step == RATE - 1)
        return carry

    lax.fori_loop(1, RATE, substep, 0)
    for q in range(quant):
        out_ref[q] = permute(state[:, col(q)], back)


def shards(
    devices,
    dofs,
    star,
    flux_minus,
    flux_plus,
    cohesion,
    stiff,
    face_proj,
    lift,
    rotate,
    cluster,
    neighbor,
    neigh_face,
    orient,
    send_elem,
    send_face,
):
    basis, quant, elems = dofs.shape
    faces, fbasis, _ = face_proj.shape
    slots = send_elem.shape[1]
    fpad = round_up(fbasis, 8)
    bpad = round_up(basis, 16)
    frows = faces * fpad
    rows = 3 * basis
    weights = np.array(
        [interval_weights(s / RATE, (s + 1) / RATE) for s in range(RATE)], np.float32
    )
    dims = (basis, quant, elems, fbasis, faces, slots)
    flat = quant * elems
    gathered = 4 * basis
    vmem = pl.BlockSpec(memory_space=pltpu.VMEM)
    arrays = [
        jnp.transpose(dofs, (1, 0, 2)),
        jnp.transpose(star, (1, 2, 0, 3)),
        jnp.transpose(flux_minus, (1, 2, 0, 3)),
        jnp.transpose(flux_plus, (1, 2, 0, 3)),
        cohesion.reshape(1, elems),
        stiff,
        jnp.transpose(face_proj, (1, 0, 2)),
        jnp.transpose(lift, (2, 0, 1)),
        rotate,
        cluster.reshape(1, elems),
        neighbor,
        neigh_face,
        orient,
        send_elem,
        send_face,
    ]
    scratch = [pltpu.VMEM(array.shape, array.dtype) for array in arrays] + [
        pltpu.SemaphoreType.DMA((len(arrays),)),
        pltpu.VMEM((3 * quant * quant, elems), F32),
        pltpu.VMEM((3 * quant * quant, elems), F32),
        pltpu.VMEM((quant * 14, elems), F32),
        pltpu.VMEM((faces * quant * quant, elems), F32),
        pltpu.VMEM((quant * faces * 5, elems), F32),
        pltpu.VMEM((faces * quant * quant, elems), F32),
        pltpu.VMEM((basis, flat), F32),
        pltpu.VMEM((round_up(rows + frows, 16), 3 * bpad), BF16),
        pltpu.VMEM((3 * frows, 3 * bpad), BF16),
        pltpu.VMEM((bpad, 2 * frows), BF16),
        pltpu.VMEM((bpad, frows), BF16),
        pltpu.VMEM((faces * elems, faces * elems), BF16),
        pltpu.VMEM((4 * slots, faces * elems), BF16),
        pltpu.VMEM((faces * elems, 4 * slots), BF16),
        pltpu.VMEM((basis, flat), F32),
        pltpu.VMEM((RATE, basis, flat), F32),
        pltpu.VMEM((basis, flat), F32),
        pltpu.VMEM((3 * bpad, flat), BF16),
        pltpu.VMEM((rows, flat), F32),
        pltpu.VMEM((rows, flat), F32),
        pltpu.VMEM((frows, flat), F32),
        pltpu.VMEM((gathered, faces * elems), F32),
        pltpu.VMEM((gathered, faces * elems), F32),
        pltpu.VMEM((frows, flat), F32),
        pltpu.VMEM((basis, flat), F32),
        pltpu.VMEM((RATE, 4, basis, 4 * slots), F32),
        pltpu.VMEM((RATE, 4, basis, 4 * slots), F32),
        pltpu.SemaphoreType.DMA((RATE, 4)),
        pltpu.SemaphoreType.DMA((RATE, 4)),
    ]
    result = pl.pallas_call(
        functools.partial(kernel, devices, dims),
        out_shape=jax.ShapeDtypeStruct((quant, basis, elems), F32),
        in_specs=[pl.BlockSpec(memory_space=pltpu.SMEM)] + [pl.BlockSpec(memory_space=pl.ANY)] * len(arrays),
        out_specs=vmem,
        scratch_shapes=scratch,
        compiler_params=pltpu.CompilerParams(
            collective_id=0, has_side_effects=True, vmem_limit_bytes=60 * 1024 * 1024
        ),
    )(
        jnp.asarray(weights),
        *arrays,
    )
    return jnp.transpose(result, (1, 0, 2))


def solution(mesh):
    placed = (
        P(None, None, "dom"),
        P(None, None, None, "dom"),
        P(None, None, None, "dom"),
        P(None, None, None, "dom"),
        P("dom"),
        P(),
        P(),
        P(),
        P(),
        P("dom"),
        P(None, "dom"),
        P(None, "dom"),
        P(None, "dom"),
        P(None, "dom"),
        P(None, "dom"),
    )
    return jax.shard_map(
        functools.partial(shards, mesh.shape["dom"]),
        mesh=mesh,
        in_specs=placed,
        out_specs=P(None, None, "dom"),
        check_vma=False,
    )
```

```python
import functools
import math

import jax
import jax.numpy as jnp
import numpy as np
from jax import lax
from jax.experimental import pallas as pl
from jax.experimental.pallas import tpu as pltpu
from jax.sharding import PartitionSpec as P

ORDER = 6
RATE = 4
OFFSETS = (-2, -1, 1, 2)
F32 = jnp.float32
BF16 = jnp.bfloat16


def round_up(value, multiple):
    return -(-value // multiple) * multiple


def interval_weights(begin_time, end_time):
    return [
        (end_time ** (term + 1) - begin_time ** (term + 1)) / math.factorial(term + 1)
        for term in range(ORDER)
    ]


def high(values):
    return values.astype(BF16).astype(F32)


def mm(left, right):
    return jnp.dot(left, right, preferred_element_type=F32)


def kernel(
    devices,
    dims,
    weight_ref,
    *refs,
):
    sources, rest = refs[:15], refs[15:]
    out_ref, rest = rest[0], rest[1:]
    loaded, rest = rest[:15], rest[15:]
    kernel_body(devices, dims, weight_ref, sources, out_ref, loaded, *rest)


def kernel_body(
    devices,
    dims,
    weight_ref,
    sources,
    out_ref,
    loaded,
    load_sem,
    sym_ref,
    sym_roll,
    sym_pack,
    minus_flat,
    minus_pack,
    minus_swapped,
    plus_flat,
    acc,
    main_ref,
    turned_ref,
    lift_high,
    lift_low,
    onehot_local,
    onehot_ghost,
    onehot_send,
    state,
    pieces,
    pred,
    rhs,
    ya,
    yb,
    own_trace,
    turned,
    remote,
    flux,
    base,
    send,
    recv,
    send_sem,
    recv_sem,
):
    basis, quant, elems, fbasis, faces, slots = dims
    (
        dofs_ref,
        star_ref,
        minus_ref,
        plus_ref,
        cohesion_ref,
        stiff_ref,
        proj_ref,
        lift_ref,
        rotate_ref,
        fine_ref,
        neighbor_ref,
        face_ref,
        orient_ref,
        send_elem_ref,
        send_face_ref,
    ) = loaded
    loads = [
        pltpu.make_async_copy(source, target, load_sem.at[i])
        for i, (source, target) in enumerate(zip(sources, loaded))
    ]
    for load in loads:
        load.start()
    fpad = round_up(fbasis, 8)
    bpad = round_up(basis, 16)
    rows = 3 * basis
    groups = [range(q, min(q + 4, quant)) for q in range(0, quant, 4)]
    frows = faces * fpad
    trows = quant * fpad
    seg = basis
    me = lax.axis_index("dom")

    def exists(position):
        other = me + OFFSETS[position]
        return (other >= 0) & (other < devices)

    barrier = pltpu.get_barrier_semaphore()
    for position in range(4):

        @pl.when(exists(position))
        def _():
            pl.semaphore_signal(
                barrier,
                inc=1,
                device_id=(me + OFFSETS[position],),
                device_id_type=pl.DeviceIdType.MESH,
            )

    def col(q):
        return slice(q * elems, (q + 1) * elems)

    def gcol(group):
        return slice(group[0] * elems, (group[-1] + 1) * elems)

    for load in loads:
        load.wait()

    half = elems // 2
    lane_id = lax.broadcasted_iota(jnp.int32, (1, elems), 1)
    left_half = lane_id < half
    row_id = lax.broadcasted_iota(jnp.int32, (elems, elems), 0)
    col_id = lax.broadcasted_iota(jnp.int32, (elems, elems), 1)
    is_fine = jnp.where(fine_ref[...] == 1, 1.0, 0.0)
    below = jnp.where(row_id <= col_id, 1.0, 0.0).astype(BF16)
    count = mm(jnp.broadcast_to(is_fine, (16, elems)).astype(BF16), below)[0:1]
    total = jnp.sum(is_fine, axis=1, keepdims=True)
    lane_f = lane_id.astype(F32)
    place_of = jnp.where(is_fine > 0.5, count - 1.0, total + lane_f - count)
    back_f = jnp.where(row_id.astype(F32) == place_of, 1.0, 0.0)
    back = back_f.astype(BF16)
    order = jnp.transpose(back_f).astype(BF16)
    fine = lane_f < total

    def permute(values, matrix):
        top = high(values)
        return mm(top.astype(BF16), matrix) + mm((values - top).astype(BF16), matrix)

    def swap(values):
        return pltpu.roll(values, half, 1)

    for c in range(3):
        for q in range(quant):
            for p in range(q, quant):
                both = 0.5 * (star_ref[q, p, c : c + 1, :] + star_ref[p, q, c : c + 1, :])
                at = (c * quant + q) * quant + p
                sym_ref[at : at + 1, :] = both
                if p != q:
                    at = (c * quant + p) * quant + q
                    sym_ref[at : at + 1, :] = both
    for q in range(quant):
        for p in range(quant):
            at = (q * quant + p) * faces
            minus_flat[at : at + faces, :] = minus_ref[q, p]
            plus_flat[at : at + faces, :] = plus_ref[q, p]
    sym_ref[...] = permute(sym_ref[...], order)
    sym_roll[...] = swap(sym_ref[...])
    minus_flat[...] = permute(minus_flat[...], order)
    plus_flat[...] = permute(plus_flat[...], order)

    minus_swapped[...] = swap(minus_flat[...])

    def sym_at(c, q, p):
        at = (c * quant + q) * quant + p
        return slice(at, at + 1)

    last_q = quant - 1
    for q in range(quant):
        for c in range(3):
            for t in range(4):
                at = q * 14 + c * 4 + t
                sym_pack[at : at + 1, :] = jnp.where(
                    left_half, sym_ref[sym_at(c, q, 2 * t), :], sym_roll[sym_at(c, q, 2 * t + 1), :]
                )
        at = q * 14 + 12
        sym_pack[at : at + 1, :] = jnp.where(
            left_half, sym_ref[sym_at(0, q, last_q), :], sym_roll[sym_at(1, q, last_q), :]
        )
        sym_pack[at + 1 : at + 2, :] = jnp.where(left_half, sym_ref[sym_at(2, q, last_q), :], 0.0)
        for f in range(faces):
            for t in range(5):
                at = (q * faces + f) * 5 + t
                one = (q * quant + 2 * t) * faces + f
                two = one + faces
                right = minus_swapped[two : two + 1, :] if t < 4 else 0.0
                minus_pack[at : at + 1, :] = jnp.where(
                    left_half, minus_flat[one : one + 1, :], right
                )

    def spread(matrix, width, offsets):
        height, count = matrix.shape
        row = lax.broadcasted_iota(jnp.int32, (count, width), 0)
        lane = lax.broadcasted_iota(jnp.int32, (count, width), 1)
        hit = lane == row + offsets[0]
        for offset in offsets[1:]:
            hit = hit | (lane == row + offset)
        place = jnp.where(hit, 1.0, 0.0).astype(BF16)
        top = high(matrix)
        return mm(top.astype(BF16), place), mm((matrix - top).astype(BF16), place)

    def left_side(matrix):
        upper, lower = spread(matrix, 3 * bpad, (0, bpad, 2 * bpad))
        lane = lax.broadcasted_iota(jnp.int32, upper.shape, 1)
        return jnp.where(lane < 2 * bpad, upper, lower)

    def pad_rows(matrix, count):
        if count == matrix.shape[0]:
            return matrix
        blank = jnp.zeros((count - matrix.shape[0], matrix.shape[1]), F32)
        return jnp.concatenate([matrix, blank], axis=0)

    projections = [pad_rows(proj_ref[:, f, :], fpad) for f in range(faces)]
    blocks = []
    for c in range(3):
        whole = stiff_ref[c]
        blocks.append(0.5 * (jnp.transpose(whole) - whole))
    blocks = jnp.concatenate(blocks + projections, axis=0)
    main_ref[...] = left_side(pad_rows(blocks, main_ref.shape[0])).astype(BF16)
    turns = jnp.concatenate([pad_rows(rotate_ref[k], fpad) for k in range(3)], axis=0)
    spins = [
        jnp.dot(
            turns,
            proj_ref[:, f, :],
            preferred_element_type=F32,
            precision=lax.Precision.HIGHEST,
        )
        for f in range(faces)
    ]
    for k in range(3):
        spun = [spin[k * fpad : (k + 1) * fpad] for spin in spins]
        turned_ref[k * frows : (k + 1) * frows, :] = left_side(
            jnp.concatenate(spun, axis=0)
        ).astype(BF16)
    upper, lower = None, None
    for f in range(faces):
        one, two = spread(
            pad_rows(jnp.transpose(pad_rows(lift_ref[:, f, :], fpad)), bpad),
            2 * frows,
            (f * fpad, frows + f * fpad),
        )
        upper = one if upper is None else upper + one
        lower = two if lower is None else lower + two
    lift_high[...] = upper.astype(BF16)
    lift_low[...] = lower[:, 0:frows].astype(BF16)

    def onehot(row_count, index):
        ids = lax.broadcasted_iota(jnp.int32, (row_count, index.shape[1]), 0)
        return jnp.where(ids == index, 1.0, 0.0).astype(BF16)

    def permuted_ids(ref):
        return mm(ref[...].astype(F32).astype(BF16), order).astype(jnp.int32)

    neighbor_ids = permuted_ids(neighbor_ref)
    face_ids = permuted_ids(face_ref)
    orient_ids = permuted_ids(orient_ref)

    def sorted_rows(f, raw):
        return mm(back, raw[f * elems : (f + 1) * elems]).astype(BF16)

    for f in range(faces):
        target = neighbor_ids[f : f + 1, :]
        across = face_ids[f : f + 1, :]
        local = jnp.where(target < elems, across * elems + target, -1)
        raw = onehot(faces * elems, local)
        for g in range(faces):
            onehot_local[g * elems : (g + 1) * elems, f * elems : (f + 1) * elems] = sorted_rows(
                g, raw
            )
        onehot_ghost[:, f * elems : (f + 1) * elems] = onehot(4 * slots, target - elems)
    slot_row = lax.broadcasted_iota(jnp.int32, (slots, 4 * slots), 0)
    slot_lane = lax.broadcasted_iota(jnp.int32, (slots, 4 * slots), 1)
    place = jnp.where(slot_lane % slots == slot_row, 1.0, 0.0).astype(BF16)
    block_row = lax.broadcasted_iota(jnp.int32, (4, 4 * slots), 0)
    block_lane = lax.broadcasted_iota(jnp.int32, (4, 4 * slots), 1) // slots

    def one_row(ref):
        wide = mm(ref[...].astype(F32).astype(BF16), place)
        return jnp.sum(jnp.where(block_lane == block_row, wide, 0.0), axis=0, keepdims=True)

    slot = one_row(send_face_ref) * elems + one_row(send_elem_ref)
    raw = onehot(faces * elems, slot.astype(jnp.int32))
    for g in range(faces):
        onehot_send[g * elems : (g + 1) * elems, :] = sorted_rows(g, raw)
    wide_cohesion = jnp.broadcast_to(cohesion_ref[...], (16, elems))
    coh_top = high(wide_cohesion)
    coh_rest = wide_cohesion - coh_top
    coh_mid = high(coh_rest)
    sorted_cohesion = (
        mm(coh_top.astype(BF16), order)
        + mm(coh_mid.astype(BF16), order)
        + mm((coh_rest - coh_mid).astype(BF16), order)
    )[0:1]


    def put(q, values):
        top = high(values)
        pad = jnp.zeros((bpad - basis, elems), F32)
        upper = jnp.concatenate([values, pad], axis=0).astype(BF16)
        lower = jnp.concatenate([values - top, pad], axis=0).astype(BF16)
        rhs[0:bpad, col(q)] = upper
        rhs[bpad : 2 * bpad, col(q)] = lower
        rhs[2 * bpad : 3 * bpad, col(q)] = upper

    skew_rows = round_up(rows, 16)

    def product(group, target):
        result = mm(main_ref[0:skew_rows, :], rhs[:, gcol(group)])
        target[:, gcol(group)] = result[0:rows]

    def stage(source, target, emit):
        for group in groups:
            sums = [None] * len(group)
            for c in range(3):
                for p in range(quant):
                    values = source[c * basis : (c + 1) * basis, col(p)]
                    for i, q in enumerate(group):
                        term = sym_ref[sym_at(c, q, p), :] * values
                        sums[i] = term if sums[i] is None else sums[i] + term
            for i, q in enumerate(group):
                emit(q, sums[i])
                if target is not None:
                    put(q, sums[i])
            if target is not None:
                product(group, target)

    tiles = ((0, 1), (2, 3), (4,))

    def tile_cols(part):
        return slice(tiles[part][0] * elems, (tiles[part][-1] + 1) * elems)

    def packed_product(part, target):
        result = mm(main_ref[0:skew_rows, :], rhs[:, tile_cols(part)])
        target[:, tile_cols(part)] = result[0:rows]

    def pack(t, values):
        if t < 4:
            put(t, jnp.where(left_half, values[0], values[1]))
        else:
            put(t, values[0])

    def packed_stage(source, target, emit):
        for part, group in enumerate(groups):
            sums = [None] * len(group)
            for k in range(14):
                if k < 12:
                    c, t = k // 4, k % 4
                    values = source[c * basis : (c + 1) * basis, col(t)]
                elif k == 12:
                    values = jnp.where(
                        left_half, source[0:basis, col(4)], source[basis : 2 * basis, col(4)]
                    )
                else:
                    values = source[2 * basis : 3 * basis, col(4)]
                for i, q in enumerate(group):
                    term = sym_pack[q * 14 + k : q * 14 + k + 1, :] * values
                    sums[i] = term if sums[i] is None else sums[i] + term
            sums = [value + swap(value) for value in sums]
            for i, q in enumerate(group):
                emit(q, sums[i])
            if target is not None:
                for i, t in enumerate(tiles[part]):
                    pack(t, sums[2 * i : 2 * i + 2])
                packed_product(part, target)

    def packed_series(emit):
        for part, group in enumerate(groups):
            both = []
            for q in group:
                value = state[:, col(q)]
                value = jnp.where(left_half, value, swap(value))
                emit(0, q, value)
                both.append(value)
            for i, t in enumerate(tiles[part]):
                pack(t, both[2 * i : 2 * i + 2])
            packed_product(part, ya)

        def pair(j, carry):
            packed_stage(ya, yb, functools.partial(emit, 2 * j + 1))
            packed_stage(yb, ya, functools.partial(emit, 2 * j + 2))
            return carry

        lax.fori_loop(0, 2, pair, 0)
        packed_stage(ya, None, functools.partial(emit, 5))

    def series(emit):
        for group in groups:
            for i, q in enumerate(group):
                emit(0, q, state[:, col(q)])
                put(q, state[:, col(q)])
            product(group, ya)

        def pair(j, carry):
            stage(ya, yb, functools.partial(emit, 2 * j + 1))
            stage(yb, ya, functools.partial(emit, 2 * j + 2))
            return carry

        lax.fori_loop(0, 2, pair, 0)
        stage(ya, None, functools.partial(emit, 5))

    def copy_of(step, position):
        return pltpu.make_async_remote_copy(
            src_ref=send.at[step, position],
            dst_ref=recv.at[step, 3 - position],
            send_sem=send_sem.at[step, position],
            recv_sem=recv_sem.at[step, 3 - position],
            device_id=(me + OFFSETS[position],),
            device_id_type=pl.DeviceIdType.MESH,
        )

    lane_seg = lax.broadcasted_iota(jnp.int32, (seg, 4 * slots), 1) // slots

    def repack(parts):
        made = []
        for b in range(4):
            value = parts[0] if b == 0 else pltpu.roll(parts[0], (4 - b) * slots, 1)
            for j in range(1, 4):
                shift = ((j - b) % 4) * slots
                moved = parts[j] if shift == 0 else pltpu.roll(parts[j], shift, 1)
                value = jnp.where(lane_seg == j, moved, value)
            made.append(value)
        return made

    def two_halves(values):
        top = high(values)
        return top.astype(BF16), (values - top).astype(BF16)

    def exchange(step, first, last):
        for group in groups:
            for i, q in enumerate(group):
                put(q, pieces[0, :, col(q)] if first else pred[:, col(q)])
            result = mm(turned_ref[...], rhs[:, gcol(group)])
            for i, q in enumerate(group):
                for f in range(faces):
                    code = orient_ids[f : f + 1, :]
                    options = [
                        result[
                            k * frows + f * fpad : k * frows + (f + 1) * fpad,
                            i * elems : (i + 1) * elems,
                        ]
                        for k in range(3)
                    ]
                    turned[q * fpad : (q + 1) * fpad, f * elems : (f + 1) * elems] = jnp.where(
                        code == 0, options[0], jnp.where(code == 1, options[2], options[1])
                    )
        top, low = two_halves(turned[...])
        sending = mm(top, onehot_send[...]) + mm(low, onehot_send[...])
        parts = [sending[j * seg : (j + 1) * seg] for j in range(4)]
        for b, value in enumerate(repack(parts)):
            send[step, b] = value
        if first:
            peers = sum(exists(position).astype(jnp.int32) for position in range(4))
            pl.semaphore_wait(barrier, peers)
        for position in range(4):

            @pl.when(exists(position))
            def _():
                copy_of(step, position).start()

        remote[...] = mm(top, onehot_local[...]) + mm(low, onehot_local[...])
        if first:
            for q in range(quant):
                whole = pieces[0, :, col(q)]
                for other in range(1, RATE):
                    whole = whole + pieces[other, :, col(q)]
                put(q, jnp.where(fine, pieces[0, :, col(q)], whole))
        else:
            for part, group in enumerate(groups):
                for i, t in enumerate(tiles[part]):
                    pack(t, [acc[:, col(q)] for q in group[2 * i : 2 * i + 2]])
        for part, group in enumerate(groups):
            lanes = gcol(group) if first else tile_cols(part)
            result = mm(main_ref[...], rhs[:, lanes])
            ya[:, lanes] = result[0:rows]
            own_trace[:, lanes] = result[rows : rows + frows]

        def volume(q, value):
            if not first:
                value = jnp.where(fine, value, 0.0)
            base[:, col(q)] = state[:, col(q)] + value

        if first:
            stage(ya, None, volume)
        else:
            packed_stage(ya, None, volume)

        def solver(matrix_ref, f, group, load):
            sums = [None] * len(group)
            for p in range(quant):
                values = load(p)
                for i, q in enumerate(group):
                    at = (q * quant + p) * faces + f
                    term = matrix_ref[at : at + 1, :] * values
                    sums[i] = term if sums[i] is None else sums[i] + term
            return sums

        def packed_solver(f, group):
            sums = [None] * len(group)
            for t in range(5):
                values = own_trace[f * fpad : (f + 1) * fpad, col(t)]
                for i, q in enumerate(group):
                    at = (q * faces + f) * 5 + t
                    term = minus_pack[at : at + 1, :] * values
                    sums[i] = term if sums[i] is None else sums[i] + term
            return [jnp.where(fine, value + swap(value), 0.0) for value in sums]

        for f in range(faces):
            frange = slice(f * fpad, (f + 1) * fpad)
            for group in groups:
                if first:
                    sums = solver(minus_flat, f, group, lambda p: own_trace[frange, col(p)])
                else:
                    sums = packed_solver(f, group)
                for i, q in enumerate(group):
                    flux[frange, col(q)] = sums[i]
        for position in range(4):

            @pl.when(exists(position))
            def _():
                copy_of(step, 3 - position).wait_recv()

        ghosts = repack([recv[step, b] for b in range(4)])
        ghost = jnp.concatenate(ghosts, axis=0)
        top, low = two_halves(ghost)
        remote[...] += mm(top, onehot_ghost[...]) + mm(low, onehot_ghost[...])
        for f in range(faces):
            frange = slice(f * fpad, (f + 1) * fpad)
            for group in groups:
                sums = solver(
                    plus_flat,
                    f,
                    group,
                    lambda p: remote[p * fpad : (p + 1) * fpad, f * elems : (f + 1) * elems],
                )
                for i, q in enumerate(group):
                    flux[frange, col(q)] += sums[i]
        for group in groups:
            top, low = two_halves(flux[:, gcol(group)])
            lifted = mm(lift_high[...], jnp.concatenate([top, low], axis=0)) + mm(
                lift_low[...], top
            )
            base[:, gcol(group)] = base[:, gcol(group)] - lifted[0:basis]
        s = [base[0:1, col(q)] for q in range(6)]
        mean = (s[0] + s[1] + s[2]) / 3.0
        d = [s[i] - mean for i in range(3)]
        second = (
            0.5 * (d[0] * d[0] + d[1] * d[1] + d[2] * d[2])
            + s[3] * s[3]
            + s[4] * s[4]
            + s[5] * s[5]
        )
        cohesion = sorted_cohesion
        factor = cohesion / jnp.maximum(jnp.sqrt(second), cohesion)
        if last is not True:
            factor = jnp.where(fine | last, factor, 1.0)
        normal = [base[:, col(q)] for q in range(3)]
        pressure = (normal[0] + normal[1] + normal[2]) / 3.0
        for q in range(3):
            state[:, col(q)] = pressure + factor * (normal[q] - pressure)
        for q in range(3, 6):
            state[:, col(q)] = factor * base[:, col(q)]
        for q in range(6, quant):
            state[:, col(q)] = base[:, col(q)]
        for position in range(4):

            @pl.when(exists(position))
            def _():
                copy_of(step, position).wait_send()

    for q in range(quant):
        state[:, col(q)] = permute(dofs_ref[q], order)
    turned[...] = jnp.zeros(turned.shape, F32)
    recv_zero = jnp.zeros((seg, 4 * slots), F32)
    for position in range(4):

        @pl.when(jnp.logical_not(exists(position)))
        def _():
            for step in range(RATE):
                recv[step, position] = recv_zero

    def first_emit(term, q, value):
        for s in range(RATE):
            part = weight_ref[s, term] * value
            if isinstance(term, int) and term == 0:
                pieces[s, :, col(q)] = part
            else:
                pieces[s, :, col(q)] += part

    series(first_emit)
    exchange(0, True, False)

    def substep(step, carry):
        def emit(term, q, value):
            part = weight_ref[0, term] * value
            if isinstance(term, int) and term == 0:
                acc[:, col(q)] = part
            else:
                acc[:, col(q)] += part

        packed_series(emit)
        for q in range(quant):
            pred[:, col(q)] = jnp.where(fine, acc[:, col(q)], pieces[step, :, col(q)])
        exchange(step, False, step == RATE - 1)
        return carry

    lax.fori_loop(1, RATE, substep, 0)
    for q in range(quant):
        out_ref[q] = permute(state[:, col(q)], back)


def shards(
    devices,
    dofs,
    star,
    flux_minus,
    flux_plus,
    cohesion,
    stiff,
    face_proj,
    lift,
    rotate,
    cluster,
    neighbor,
    neigh_face,
    orient,
    send_elem,
    send_face,
):
    basis, quant, elems = dofs.shape
    faces, fbasis, _ = face_proj.shape
    slots = send_elem.shape[1]
    fpad = round_up(fbasis, 8)
    bpad = round_up(basis, 16)
    frows = faces * fpad
    rows = 3 * basis
    weights = np.array(
        [interval_weights(s / RATE, (s + 1) / RATE) for s in range(RATE)], np.float32
    )
    dims = (basis, quant, elems, fbasis, faces, slots)
    flat = quant * elems
    gathered = 4 * basis
    vmem = pl.BlockSpec(memory_space=pltpu.VMEM)
    arrays = [
        jnp.transpose(dofs, (1, 0, 2)),
        jnp.transpose(star, (1, 2, 0, 3)),
        jnp.transpose(flux_minus, (1, 2, 0, 3)),
        jnp.transpose(flux_plus, (1, 2, 0, 3)),
        cohesion.reshape(1, elems),
        stiff,
        jnp.transpose(face_proj, (1, 0, 2)),
        jnp.transpose(lift, (2, 0, 1)),
        rotate,
        cluster.reshape(1, elems),
        neighbor,
        neigh_face,
        orient,
        send_elem,
        send_face,
    ]
    scratch = [pltpu.VMEM(array.shape, array.dtype) for array in arrays] + [
        pltpu.SemaphoreType.DMA((len(arrays),)),
        pltpu.VMEM((3 * quant * quant, elems), F32),
        pltpu.VMEM((3 * quant * quant, elems), F32),
        pltpu.VMEM((quant * 14, elems), F32),
        pltpu.VMEM((faces * quant * quant, elems), F32),
        pltpu.VMEM((quant * faces * 5, elems), F32),
        pltpu.VMEM((faces * quant * quant, elems), F32),
        pltpu.VMEM((faces * quant * quant, elems), F32),
        pltpu.VMEM((basis, flat), F32),
        pltpu.VMEM((round_up(rows + frows, 16), 3 * bpad), BF16),
        pltpu.VMEM((3 * frows, 3 * bpad), BF16),
        pltpu.VMEM((bpad, 2 * frows), BF16),
        pltpu.VMEM((bpad, frows), BF16),
        pltpu.VMEM((faces * elems, faces * elems), BF16),
        pltpu.VMEM((4 * slots, faces * elems), BF16),
        pltpu.VMEM((faces * elems, 4 * slots), BF16),
        pltpu.VMEM((basis, flat), F32),
        pltpu.VMEM((RATE, basis, flat), F32),
        pltpu.VMEM((basis, flat), F32),
        pltpu.VMEM((3 * bpad, flat), BF16),
        pltpu.VMEM((rows, flat), F32),
        pltpu.VMEM((rows, flat), F32),
        pltpu.VMEM((frows, flat), F32),
        pltpu.VMEM((gathered, faces * elems), F32),
        pltpu.VMEM((gathered, faces * elems), F32),
        pltpu.VMEM((frows, flat), F32),
        pltpu.VMEM((basis, flat), F32),
        pltpu.VMEM((RATE, 4, basis, 4 * slots), F32),
        pltpu.VMEM((RATE, 4, basis, 4 * slots), F32),
        pltpu.SemaphoreType.DMA((RATE, 4)),
        pltpu.SemaphoreType.DMA((RATE, 4)),
    ]
    result = pl.pallas_call(
        functools.partial(kernel, devices, dims),
        out_shape=jax.ShapeDtypeStruct((quant, basis, elems), F32),
        in_specs=[pl.BlockSpec(memory_space=pltpu.SMEM)] + [pl.BlockSpec(memory_space=pl.ANY)] * len(arrays),
        out_specs=vmem,
        scratch_shapes=scratch,
        compiler_params=pltpu.CompilerParams(
            collective_id=0, has_side_effects=True, vmem_limit_bytes=60 * 1024 * 1024
        ),
    )(
        jnp.asarray(weights),
        *arrays,
    )
    return jnp.transpose(result, (1, 0, 2))


def solution(mesh):
    placed = (
        P(None, None, "dom"),
        P(None, None, None, "dom"),
        P(None, None, None, "dom"),
        P(None, None, None, "dom"),
        P("dom"),
        P(),
        P(),
        P(),
        P(),
        P("dom"),
        P(None, "dom"),
        P(None, "dom"),
        P(None, "dom"),
        P(None, "dom"),
        P(None, "dom"),
    )
    return jax.shard_map(
        functools.partial(shards, mesh.shape["dom"]),
        mesh=mesh,
        in_specs=placed,
        out_specs=P(None, None, "dom"),
        check_vma=False,
    )
```
